32 devices in a mesh: grp: 2 (over x), seq: 16 (over z, y, core).
Axes of the slice: x: 2, y: 2, z: 4, core: 2. Of those that a mesh axis runs over, the one named last changes fastest.
Arguments:
- hidden: bfloat16 [16384, 4096], P(('grp', 'seq')), parts along dimension 0, may hold values from -6 to 6
- token_ids: int32 [32, 512], P(('grp', 'seq')), parts along dimension 0, may hold values from 0 to 128255, as said below
- upstream: bfloat16 [16384, 1024], P(('grp', 'seq')), parts along dimension 0, may hold values from -6 to 6
- w_value: bfloat16 [4096, 1024], P('seq'), may hold values from -0.09375 to 0.09375
- proj_in: bfloat16 [4096, 64], replicated, may hold values from -0.09375 to 0.09375
- proj_out: bfloat16 [8, 128, 64], replicated, may hold values from -0.5 to 0.5
- in_inverse: float32 [8, 64, 64], replicated
- out_inverse: float32 [8, 64, 64], replicated
- datastore: bfloat16 [1024, 32768], P(('grp', 'seq')), parts along dimension 0
Outputs:
- input_grad: bfloat16 [16384, 4096], P(('grp', 'seq')), parts along dimension 0
- scores: float32 [32, 512], P('grp', 'seq'), parts along dimension 0
The draws below stay inside these ranges and needn't reach their ends.
There are 2 independent parts, one for each index of `grp`. The reference program is written for one: setup_inputs(seed, part) draws one part's arguments, and reference() takes and returns one part's arrays. A program takes and returns all parts, laid end to end along the dimension named above; an argument that names none is the same for every part. Nothing has to cross between parts.
Inputs may be any that keep to these rules, and one draw needn't show every extreme that they name: `token_ids`: each sequence holds its live tokens first, then padding ids 0; at least 128 tokens of every sequence are live and some sequence has no padding.
All inputs are finite; a program needn't handle non-finite values.
Results may differ from the reference program's by a relative error of at most 0.0059.
Values may be sent and summed in bfloat16 or wider, within the bound.
No kernel may reach another device: no remote copies, remote signals or barrier semaphores. Data moves between devices by JAX's collectives and lax.ppermute only.
A program may use at most 128 MiB of HBM per device.

```python
import jax
import jax.numpy as jnp
from jax import lax

D = 4096
KVH = 8
HD = 128
RANK = 64
TOK = 512
KV = 1024
FLAT = 32768
QUERIES = 16
DS_ROWS = 512


def draw_token_ids(key, part):
    key_len = jax.random.fold_in(key, 11)
    key_ids = jax.random.fold_in(key, 12)
    key_full = jax.random.fold_in(key, 13)
    lengths = jax.random.randint(key_len, (QUERIES,), TOK // 4, TOK + 1)
    full_row = jax.random.randint(key_full, (), 0, QUERIES)
    lengths = lengths.at[full_row].set(TOK)
    ids_drawn = jax.random.randint(key_ids, (QUERIES, TOK), 1, 128256)
    ids_drawn = ids_drawn.at[full_row, 0].set(128255)
    position = jnp.arange(TOK, dtype=jnp.int32)[None, :]
    return jnp.where(position < lengths[:, None], ids_drawn, 0).astype(jnp.int32)


def inverse_factor(key):
    key_diag = jax.random.fold_in(key, 21)
    key_off = jax.random.fold_in(key, 22)
    diag_vals = jax.random.uniform(key_diag, (KVH, RANK), jnp.float32, 1.0, 2.0)
    noise = jax.random.normal(key_off, (KVH, RANK, RANK), jnp.float32)
    noise = 0.5 * (noise + jnp.swapaxes(noise, 1, 2)) / jnp.sqrt(2.0 * RANK)
    eye_mat = jnp.eye(RANK, dtype=jnp.float32)[None]
    return eye_mat * diag_vals[:, :, None] + noise


def draw_in_inverse(key, part):
    return inverse_factor(jax.random.fold_in(key, 31))


def draw_out_inverse(key, part):
    return inverse_factor(jax.random.fold_in(key, 32))


def draw_datastore(key, part):
    key_val = jax.random.fold_in(key, 41)
    key_row = jax.random.fold_in(key, 42)
    row_pos = jnp.arange(DS_ROWS, dtype=jnp.float32) / DS_ROWS
    row_scale = jnp.exp(jax.random.uniform(key_row, (DS_ROWS,), jnp.float32, 0.0, 2.3026)) * jnp.exp(1.0986 * row_pos)
    values = jax.random.normal(key_val, (DS_ROWS, FLAT), jnp.float32)
    return (values * row_scale[:, None]).astype(jnp.bfloat16)


def block_levels(key, extent, shards, smallest, top_value):
    loudness = 1.0
    for dim, shards_of in shards:
        steps = jax.random.uniform(jax.random.fold_in(jax.random.fold_in(key, 6), dim), (shards_of,), jnp.float32, smallest / len(shards), top_value / len(shards))
        loudness = loudness * jnp.repeat(jnp.exp(steps), extent[dim] // shards_of).reshape((-1,) + (1,) * (len(extent) - 1 - dim))
    return loudness


def scatter_about(own_key, shape, scale, most, split=(), held_as=jnp.bfloat16):
    factor_of = block_levels(own_key, shape, split, -0.22, 0.18) if split else 1.0
    values = jax.random.normal(own_key, shape, jnp.float32) * scale * factor_of
    return jnp.minimum(jnp.maximum(values, -most), most).astype(held_as)


def setup_inputs(seed: int = 0, part: int = 0) -> dict:
    streams_of = jax.random.split(jax.random.key(seed), 10)
    part_splits = jax.random.split(jax.random.fold_in(streams_of[9], part), 10)
    return {
        "hidden": scatter_about(part_splits[0], (QUERIES * TOK, D), 1.0, 6.0, ((0, 16),)),
        "token_ids": draw_token_ids(jax.random.fold_in(jax.random.fold_in(streams_of[9], part), 71), part),
        "upstream": scatter_about(part_splits[2], (QUERIES * TOK, KV), 1.0, 6.0, ((0, 16),)),
        "w_value": scatter_about(streams_of[3], (D, KV), D ** -0.5, 0.09375, ((0, 16),)),
        "proj_in": scatter_about(streams_of[4], (D, RANK), D ** -0.5, 0.09375),
        "proj_out": scatter_about(streams_of[5], (KVH, HD, RANK), HD ** -0.5, 0.5),
        "in_inverse": draw_in_inverse(jax.random.fold_in(streams_of[9], 71), part),
        "out_inverse": draw_out_inverse(jax.random.fold_in(streams_of[9], 71), part),
        "datastore": draw_datastore(jax.random.fold_in(jax.random.fold_in(streams_of[9], part), 71), part),
    }


def reference(hidden, token_ids, upstream, w_value, proj_in, proj_out, in_inverse, out_inverse, datastore):
    live_mask = (token_ids != 0).reshape(-1, 1).astype(jnp.bfloat16)
    masked = upstream * live_mask
    input_grad = jnp.dot(masked, w_value.T, preferred_element_type=jnp.float32).astype(jnp.bfloat16)
    left_proj = jnp.dot(hidden, proj_in, preferred_element_type=jnp.float32).astype(jnp.bfloat16)
    cot_heads = masked.reshape(-1, KVH, HD).astype(jnp.float32)
    right_proj = jnp.einsum('thd,hdr->thr', cot_heads, proj_out.astype(jnp.float32)).astype(jnp.bfloat16)
    left_seq = left_proj.astype(jnp.float32).reshape(QUERIES, TOK, RANK)
    right_seq = right_proj.astype(jnp.float32).reshape(QUERIES, TOK, KVH, RANK)
    raw_grads = jnp.einsum('qti,qthj->qhij', left_seq, right_seq)
    half_way = jnp.einsum('hai,qhij->qhaj', in_inverse, raw_grads, precision=lax.Precision.HIGHEST)
    pre_grads = jnp.einsum('qhaj,hjb->qhab', half_way, out_inverse, precision=lax.Precision.HIGHEST)
    query_grads = pre_grads.astype(jnp.bfloat16).reshape(QUERIES, FLAT)
    raw_scores = jnp.dot(query_grads, datastore.T, preferred_element_type=jnp.float32)
    spread = jnp.sqrt(lax.optimization_barrier(jnp.mean(raw_scores * raw_scores, axis=1, keepdims=True)) + 1e-06)
    return (input_grad, raw_scores / spread)
```

```python
import functools

import jax
import jax.numpy as jnp
from jax import lax
from jax.experimental import pallas as pl
from jax.experimental.pallas import tpu as pltpu
from jax.sharding import PartitionSpec as P

BF16 = jnp.bfloat16
F32 = jnp.float32
HIGHEST = lax.Precision.HIGHEST
LAST = (((1,), (1,)), ((), ()))
FIRST = (((0,), (0,)), ((), ()))
VMEM = pltpu.VMEM
VMEM_LIMIT = 40 * 1024 * 1024


def params(**more):
    return pltpu.CompilerParams(vmem_limit_bytes=VMEM_LIMIT, **more)


def grad_kernel(ids, up, hid, pin, pout, a_inv, b_inv, masked, grad, left):
    step = pl.program_id(0)
    part = lax.dot_general(hid[...], pin[...], LAST, preferred_element_type=F32)

    @pl.when(step == 0)
    def _():
        left[...] = part
        live = jnp.sum((ids[...] != 0).astype(jnp.int32))
        row = lax.broadcasted_iota(jnp.int32, up.shape, 0)
        masked[...] = jnp.where(row < live, up[...].astype(F32), 0.0).astype(BF16)

    @pl.when(step > 0)
    def _():
        left[...] += part

    @pl.when(step == pl.num_programs(0) - 1)
    def _():
        heads, rank, head_dim = pout.shape
        left_t = left[...].T.astype(BF16)
        both = jnp.dot(left_t, masked[...], preferred_element_type=F32)
        for h in range(heads):
            out_side = lax.dot_general(
                pout[h].astype(F32), b_inv[h], FIRST, precision=HIGHEST, preferred_element_type=F32
            )
            mid = jnp.dot(
                both[:, h * head_dim : (h + 1) * head_dim],
                out_side,
                precision=HIGHEST,
                preferred_element_type=F32,
            )
            pre = jnp.dot(a_inv[h], mid, precision=HIGHEST, preferred_element_type=F32)
            half = rank // 2
            rows = slice(h * half, (h + 1) * half)
            grad[rows, :] = jnp.concatenate([pre[:half], pre[half:]], axis=1).astype(BF16)


def query_gradient(token_ids, upstream, hidden, proj_in, proj_out, in_inverse, out_inverse):
    tokens, width = hidden.shape
    heads, head_dim, rank = proj_out.shape
    kv = upstream.shape[1]
    steps = 4 if width % 512 == 0 else 1
    a_inv = in_inverse.reshape(heads, rank // 2, 2, rank).swapaxes(1, 2).reshape(heads, rank, rank)
    whole = lambda *shape: pl.BlockSpec(shape, lambda i: (0,) * len(shape))
    return pl.pallas_call(
        grad_kernel,
        grid=(steps,),
        in_specs=[
            whole(*token_ids.shape),
            whole(tokens, kv),
            pl.BlockSpec((tokens, width // steps), lambda i: (0, i)),
            pl.BlockSpec((rank, width // steps), lambda i: (0, i)),
            whole(heads, rank, head_dim),
            whole(heads, rank, rank),
            whole(heads, rank, rank),
        ],
        out_specs=[whole(tokens, kv), whole(heads * rank // 2, 2 * rank)],
        out_shape=[
            jax.ShapeDtypeStruct((tokens, kv), BF16),
            jax.ShapeDtypeStruct((heads * rank // 2, 2 * rank), BF16),
        ],
        scratch_shapes=[VMEM((tokens, rank), F32)],
        compiler_params=params(),
        cost_estimate=pl.CostEstimate(
            flops=2 * tokens * width * rank,
            bytes_accessed=2 * tokens * (width + 2 * kv),
            transcendentals=0,
        ),
        name="query_gradient",
    )(
        token_ids,
        upstream,
        hidden,
        proj_in.T,
        proj_out.swapaxes(1, 2),
        a_inv,
        out_inverse,
    )


def score_kernel(place, mine, other, store, scores, power, wide):
    count = mine.shape[0]
    queries, groups = 2 * count, mine.shape[1]
    for half, ref in enumerate((mine, other)):
        for k in range(count):
            wide[pl.ds(place[half * count + k], groups, stride=queries), :] = ref[k].astype(F32)
    total = jnp.zeros(scores.shape, F32)
    lhs = jnp.concatenate(
        [wide[g * queries : (g + 1) * queries, :].astype(BF16) for g in range(groups)], axis=1
    )
    total = lax.dot_general(lhs, store[...], LAST, preferred_element_type=F32)
    scores[...] = total
    square = jnp.sum(total * total, axis=1, keepdims=True)
    power[...] = jnp.broadcast_to(square, power.shape)


def raw_score_call(place, mine, other, datastore):
    count, groups, lanes = mine.shape
    queries, rows = 2 * count, datastore.shape[0]
    vmem = pl.BlockSpec(memory_space=VMEM)
    return pl.pallas_call(
        score_kernel,
        in_specs=[pl.BlockSpec(memory_space=pltpu.SMEM), vmem, vmem, vmem],
        out_specs=[vmem, vmem],
        out_shape=[
            jax.ShapeDtypeStruct((queries, rows), F32),
            jax.ShapeDtypeStruct((queries, lanes), F32),
        ],
        scratch_shapes=[VMEM((groups * queries, lanes), F32)],
        compiler_params=params(),
        cost_estimate=pl.CostEstimate(
            flops=2 * queries * rows * groups * lanes,
            bytes_accessed=2 * (queries + rows) * groups * lanes,
            transcendentals=0,
        ),
        name="raw_scores",
    )(place, mine, other, datastore)


def column_kernel(sizes, place, *refs):
    shards, given, fresh = sizes
    half_refs, refs = refs[: 2 * shards], refs[2 * shards :]
    if shards:
        (mine, other), refs = refs[:2], refs[2:]
    came, refs = refs[:given], refs[given:]
    if not fresh:
        refs = refs[1:]
    out, refs = refs[0], refs[1:]
    if shards:
        away, weight, tile, sems = refs
    else:
        (sems,) = refs
    copies = []
    at = 1 + shards
    for ref in came:
        for k in range(ref.shape[0]):
            width = ref.shape[2]
            col = pl.multiple_of(place[at] * width, width)
            at += 1
            copy = pltpu.make_async_copy(ref.at[k], out.at[:, pl.ds(col, width)], sems.at[len(copies)])
            copy.start()
            copies.append(copy)
    for k in range(shards):
        first, second = half_refs[2 * k], half_refs[2 * k + 1]
        rows = first.shape[0]
        near = pl.multiple_of(place[0] * rows, rows)
        weight[k, pl.ds(near, rows), :] = first[...]
        weight[k, pl.ds(rows - near, rows), :] = second[...]
        tile[k] = lax.dot_general(
            mine[...], weight[k], LAST, preferred_element_type=F32
        ).astype(BF16)
        width = 2 * rows
        col = pl.multiple_of(place[1 + k] * width, width)
        copy = pltpu.make_async_copy(tile.at[k], out.at[:, pl.ds(col, width)], sems.at[len(copies)])
        copy.start()
        copies.append(copy)
        away[k] = lax.dot_general(
            other[...], weight[k], LAST, preferred_element_type=F32
        ).astype(BF16)
    for copy in copies:
        copy.wait()


def columns(name, place, halves, masked, came, out, out_shape):
    shards, given = len(halves) // 2, len(came)
    vmem, hbm = pl.BlockSpec(memory_space=VMEM), pl.BlockSpec(memory_space=pl.ANY)
    tokens = out_shape[0]
    in_specs = [pl.BlockSpec(memory_space=pltpu.SMEM)] + [vmem] * (len(halves) + len(masked) + given)
    operands = [place, *halves, *masked, *came]
    aliases = {}
    if out is not None:
        aliases = {len(operands): 0}
        operands.append(out)
        in_specs.append(hbm)
    outs, out_specs, scratch = [jax.ShapeDtypeStruct(out_shape, BF16)], [hbm], []
    moves = sum(r.shape[0] for r in came)
    flops = 0
    if shards:
        rows, depth = halves[0].shape
        outs.append(jax.ShapeDtypeStruct((shards, tokens, 2 * rows), BF16))
        out_specs.append(vmem)
        scratch = [VMEM((shards, 2 * rows, depth), BF16), VMEM((shards, tokens, 2 * rows), BF16)]
        moves += shards
        flops = 2 * shards * (2 * tokens) * (2 * rows) * depth
    return pl.pallas_call(
        functools.partial(column_kernel, (shards, given, out is None)),
        in_specs=in_specs,
        out_specs=out_specs,
        out_shape=outs,
        scratch_shapes=[*scratch, pltpu.SemaphoreType.DMA((moves,))],
        input_output_aliases=aliases,
        compiler_params=params(),
        cost_estimate=pl.CostEstimate(flops=flops, bytes_accessed=1 << 20, transcendentals=0),
        name=name,
    )(*operands)


def swap(value, axis, size, bits):
    return lax.ppermute(value, axis, [(i, i ^ bits) for i in range(size)])


def by_exchange(
    size, hidden, token_ids, upstream, w_value, proj_in, proj_out, in_inverse, out_inverse, datastore
):
    ring = functools.partial(lambda bits, v: swap(v, "seq", size, bits))
    core, side = 1, 2
    far = [4 * k for k in range(1, size // 4)]
    cross = lambda v: swap(v, "grp", 2, 1)
    me, grp = lax.axis_index("seq"), lax.axis_index("grp")
    half = w_value.shape[0] // 2
    out_shape = (hidden.shape[0], w_value.shape[0] * size)

    with jax.named_scope("weight_halves"):
        near = lax.dynamic_slice_in_dim(w_value, grp * half, half, 0)
        away = lax.dynamic_slice_in_dim(w_value, (1 - grp) * half, half, 0)
    masked, grad = query_gradient(
        token_ids, upstream, hidden, proj_in, proj_out, in_inverse, out_inverse
    )
    masked_other = ring(core, masked)

    with jax.named_scope("query_exchange"):
        line = jnp.stack([grad] + [ring(b, grad) for b in far])
        plane = jnp.concatenate([line, ring(side, line)])
        sibling = ring(core, plane)
        order = [s ^ b for s in (0, side) for b in [0] + far]
        place = jnp.stack([me ^ b for b in order] + [me ^ b ^ core for b in order])
    raw, power = raw_score_call(place.astype(jnp.int32), plane, sibling, datastore)

    with jax.named_scope("weight_exchange"):
        halves = {0: (near, away)}
        got = {b: ring(b, near) for b in far}
        first = ring(side, near)
        halves[side] = (first, cross(first))
        for b in far:
            h = got[b]
            x = cross(h)
            y = ring(side, h)
            d = cross(y)
            halves[b] = (h, x)
            halves[b ^ side] = (y, d)

    with jax.named_scope("input_grad"):
        out, came, came_from = None, [], []
        stages = [[0, side, far[0], far[0] ^ side]] + [[b, b ^ side] for b in far[1:]] + [[]]
        for n, stage in enumerate(stages):
            spots = jnp.stack([grp] + [me ^ b for b in stage] + [me ^ core ^ b for b in came_from])
            made = columns(
                f"columns_{n}",
                spots.astype(jnp.int32),
                [p for b in stage for p in halves[b]],
                [masked, masked_other] if stage else [],
                came,
                out,
                out_shape,
            )
            out = made[0]
            if stage:
                came, came_from = [ring(core, made[1])], stage

    with jax.named_scope("power"):
        bit = 1
        while bit < size:
            power = power + ring(bit, power)
            bit *= 2
        spread = jnp.sqrt(power[:, :1] / (datastore.shape[0] * size) + 1e-06)
    return out, raw / spread


def by_gather(
    size, hidden, token_ids, upstream, w_value, proj_in, proj_out, in_inverse, out_inverse, datastore
):
    queries, seq_tokens = token_ids.shape
    heads, head_dim, rank = proj_out.shape
    live_mask = (token_ids != 0).reshape(-1, 1).astype(BF16)
    masked = upstream * live_mask
    full_weight = lax.all_gather(w_value, "seq", axis=0, tiled=True)
    input_grad = lax.dot_general(masked, full_weight, LAST, preferred_element_type=F32).astype(BF16)
    left = jnp.dot(hidden, proj_in, preferred_element_type=F32).astype(BF16)
    right = jnp.einsum(
        "thd,hdr->thr", masked.reshape(-1, heads, head_dim), proj_out, preferred_element_type=F32
    ).astype(BF16)
    raw_grads = jnp.einsum(
        "qti,qthj->qhij",
        left.reshape(queries, seq_tokens, rank),
        right.reshape(queries, seq_tokens, heads, rank),
        preferred_element_type=F32,
    )
    half_way = jnp.einsum("hai,qhij->qhaj", in_inverse, raw_grads, precision=HIGHEST)
    pre = jnp.einsum("qhaj,hjb->qhab", half_way, out_inverse, precision=HIGHEST)
    grads = pre.astype(BF16).reshape(queries, -1)
    raw = lax.dot_general(
        lax.all_gather(grads, "seq", axis=0, tiled=True),
        datastore,
        LAST,
        preferred_element_type=F32,
    )
    power = lax.psum(jnp.sum(raw * raw, axis=1), "seq")
    spread = jnp.sqrt(power / (datastore.shape[0] * size) + 1e-06)
    return input_grad, raw / spread[:, None]


def solution(mesh):
    size, groups = mesh.shape["seq"], mesh.shape["grp"]

    def on_device(*args):
        hidden, token_ids, upstream, w_value = args[:4]
        fits = (
            groups == 2
            and size >= 8
            and size & (size - 1) == 0
            and token_ids.shape[0] == 1
            and w_value.shape[0] % 256 == 0
        )
        return (by_exchange if fits else by_gather)(size, *args)

    rows = P(("grp", "seq"), None)
    return jax.shard_map(
        on_device,
        mesh=mesh,
        in_specs=(rows, rows, rows, P("seq", None), P(), P(), P(), P(), rows),
        out_specs=(rows, P("grp", "seq")),
        check_vma=False,
    )
```

```python
import functools

import jax
import jax.numpy as jnp
from jax import lax
from jax.experimental import pallas as pl
from jax.experimental.pallas import tpu as pltpu
from jax.sharding import PartitionSpec as P

BF16 = jnp.bfloat16
F32 = jnp.float32
HIGHEST = lax.Precision.HIGHEST
LAST = (((1,), (1,)), ((), ()))
FIRST = (((0,), (0,)), ((), ()))
VMEM = pltpu.VMEM
MIB = 1024 * 1024


SMALL = pl.CostEstimate(flops=1, bytes_accessed=1, transcendentals=0)


def params(mib=24):
    return pltpu.CompilerParams(vmem_limit_bytes=mib * MIB)


def split(x):
    high = x.astype(BF16)
    return high, (x - high.astype(F32)).astype(BF16)


def mask_kernel(ids, up, masked):
    live = jnp.sum((ids[...] != 0).astype(jnp.int32))
    row = lax.broadcasted_iota(jnp.int32, up.shape, 0)
    masked[...] = jnp.where(row < live, up[...].astype(F32), 0.0).astype(BF16)


def mask(token_ids, upstream):
    return pl.pallas_call(
        mask_kernel,
        in_specs=[pl.BlockSpec(memory_space=VMEM)] * 2,
        out_specs=pl.BlockSpec(memory_space=VMEM),
        out_shape=jax.ShapeDtypeStruct(upstream.shape, BF16),
        compiler_params=params(),
        cost_estimate=SMALL,
        name="mask",
    )(token_ids, upstream)


def grad_kernel(ids, pout, a_inv, b_inv, up_hbm, hid_hbm, pin_hbm, masked, grad, up, hid, pin, sems):
    steps, _, chunk = hid.shape
    copies = [pltpu.make_async_copy(pin_hbm, pin, sems.at[0])]
    for k in range(steps):
        copies.append(
            pltpu.make_async_copy(hid_hbm.at[:, pl.ds(k * chunk, chunk)], hid.at[k], sems.at[1 + k])
        )
    copies.append(pltpu.make_async_copy(up_hbm, up, sems.at[1 + steps]))
    for copy in copies:
        copy.start()
    heads, rank, head_dim = pout.shape
    half = rank // 2
    out_sides, in_sides = [], []
    for h in range(heads):
        high, low = split(b_inv[h])
        side = lax.dot_general(pout[h], high, FIRST, preferred_element_type=F32)
        side += lax.dot_general(pout[h], low, FIRST, preferred_element_type=F32)
        high, low = split(side)
        out_sides.append(jnp.concatenate([high, low, high], axis=0))
        rows = [a_inv[h, pl.ds(odd, half, stride=2), :] for odd in range(2)]
        high, low = split(jnp.concatenate(rows, axis=0))
        in_sides.append(jnp.concatenate([high, high, low], axis=1))
    copies[0].wait()
    left = None
    for k in range(steps):
        copies[1 + k].wait()
        part = lax.dot_general(
            hid[k], pin[:, k * chunk : (k + 1) * chunk], LAST, preferred_element_type=F32
        )
        left = part if left is None else left + part
    copies[-1].wait()
    mask_kernel(ids, up, masked)
    both = jnp.dot(left.T.astype(BF16), masked[...], preferred_element_type=F32)
    high, low = split(both)
    for h in range(heads):
        lanes = slice(h * head_dim, (h + 1) * head_dim)
        terms = jnp.concatenate([high[:, lanes], high[:, lanes], low[:, lanes]], axis=1)
        mid = jnp.dot(terms, out_sides[h], preferred_element_type=F32)
        mid_high, mid_low = split(mid)
        terms = jnp.concatenate([mid_high, mid_low, mid_high], axis=0)
        pre = jnp.dot(in_sides[h], terms, preferred_element_type=F32)
        grad[h * half : (h + 1) * half, :] = jnp.concatenate(
            [pre[:half], pre[half:]], axis=1
        ).astype(BF16)


def query_gradient(token_ids, upstream, hidden, proj_in, proj_out, in_inverse, out_inverse):
    tokens, width = hidden.shape
    heads, head_dim, rank = proj_out.shape
    steps = 4 if width % 512 == 0 else 1
    vmem, hbm = pl.BlockSpec(memory_space=VMEM), pl.BlockSpec(memory_space=pltpu.HBM)
    whole = pl.BlockSpec()
    return pl.pallas_call(
        grad_kernel,
        in_specs=[whole] * 4 + [hbm] * 3,
        out_specs=[vmem, vmem],
        out_shape=[
            jax.ShapeDtypeStruct(upstream.shape, BF16),
            jax.ShapeDtypeStruct((heads * rank // 2, 2 * rank), BF16),
        ],
        scratch_shapes=[
            VMEM(upstream.shape, BF16),
            VMEM((steps, tokens, width // steps), BF16),
            VMEM((rank, width), BF16),
            pltpu.SemaphoreType.DMA((steps + 2,)),
        ],
        compiler_params=params(57),
        cost_estimate=SMALL,
        name="query_gradient",
    )(token_ids, proj_out.swapaxes(1, 2), in_inverse, out_inverse, upstream, hidden, proj_in.T)


def join_kernel(first, second, both):
    count = first.shape[0]
    both[:count] = first[...]
    both[count:] = second[...]


def join(first, second):
    vmem = pl.BlockSpec(memory_space=VMEM)
    shape = (first.shape[0] + second.shape[0], *first.shape[1:])
    return pl.pallas_call(
        join_kernel,
        in_specs=[vmem, vmem],
        out_specs=vmem,
        out_shape=jax.ShapeDtypeStruct(shape, first.dtype),
        compiler_params=params(),
        cost_estimate=SMALL,
        name="join",
    )(first, second)


def score_kernel(bits, *refs):
    *held, store_hbm, scores, power, wide, store, sems = refs
    steps, _, chunk = store.shape
    copies = []
    for k in range(steps):
        copies.append(
            pltpu.make_async_copy(store_hbm.at[:, pl.ds(k * chunk, chunk)], store.at[k], sems.at[k])
        )
        copies[-1].start()
    me = lax.axis_index("seq")
    queries = len(bits)
    groups, lanes = held[0].shape[1:]
    rows = [ref.at[k] for ref in held for k in range(ref.shape[0])]
    for bit, row in zip(bits, rows):
        wide[pl.ds(me ^ bit, groups, stride=queries), :] = row[...].astype(F32)
    total = jnp.zeros(scores.shape, F32)
    each = chunk // lanes
    for k in range(steps):
        lhs = jnp.concatenate(
            [
                wide[g * queries : (g + 1) * queries, :].astype(BF16)
                for g in range(k * each, (k + 1) * each)
            ],
            axis=1,
        )
        copies[k].wait()
        total += lax.dot_general(lhs, store[k], LAST, preferred_element_type=F32)
    scores[...] = total
    square = jnp.sum(total * total, axis=1, keepdims=True)
    power[...] = jnp.broadcast_to(square, power.shape)


def raw_score_call(bits, held, datastore):
    groups, lanes = held[0].shape[1:]
    queries, (rows, flat) = len(bits), datastore.shape
    steps = 4 if groups % 4 == 0 else 1
    vmem = pl.BlockSpec(memory_space=VMEM)
    return pl.pallas_call(
        functools.partial(score_kernel, bits),
        in_specs=[vmem] * len(held) + [pl.BlockSpec(memory_space=pltpu.HBM)],
        out_specs=[vmem, vmem],
        out_shape=[
            jax.ShapeDtypeStruct((queries, rows), F32),
            jax.ShapeDtypeStruct((queries, lanes), F32),
        ],
        scratch_shapes=[
            VMEM((groups * queries, lanes), F32),
            VMEM((steps, rows, flat // steps), BF16),
            pltpu.SemaphoreType.DMA((steps,)),
        ],
        compiler_params=params(48),
        cost_estimate=SMALL,
        name="raw_scores",
    )(*held, datastore)


def put(source, out, spot, sem):
    width = source.shape[1]
    col = pl.multiple_of(spot * width, width)
    copy = pltpu.make_async_copy(source, out.at[:, pl.ds(col, width)], sem)
    copy.start()
    return copy


def column_kernel(bits, pieces, fresh, mine, other, *refs):
    me, grp = lax.axis_index("seq"), lax.axis_index("grp")
    shard_refs = []
    for count, _ in pieces:
        shard_refs.append(refs[:count])
        refs = refs[count:]
    out, *away, weight, tile, sems = refs[0 if fresh else 1 :]
    copies = []
    for k, (bit, parts) in enumerate(zip(bits, shard_refs)):
        if len(parts) == 1:
            (whole,) = parts
        else:
            whole = weight.at[k]
            rows = parts[0].shape[0]
            for part, half in zip(parts, (grp, 1 - grp) if pieces[k][1] else (0, 1)):
                whole[pl.ds(pl.multiple_of(half * rows, rows), rows), :] = part[...]
        tile[k] = lax.dot_general(mine[...], whole[...], LAST, preferred_element_type=F32).astype(BF16)
        copies.append(put(tile.at[k], out, me ^ bit, sems.at[k]))
        away[k][...] = lax.dot_general(
            other[...], whole[...], LAST, preferred_element_type=F32
        ).astype(BF16)
    for copy in copies:
        copy.wait()


def columns(name, bits, tokens, shards, out, out_shape):
    vmem, hbm = pl.BlockSpec(memory_space=VMEM), pl.BlockSpec(memory_space=pltpu.HBM)
    shards, own_first = [s[0] for s in shards], [s[1] for s in shards]
    parts = [p for shard in shards for p in shard]
    operands = [*tokens, *parts]
    in_specs = [vmem] * len(operands)
    aliases = {}
    if out is not None:
        aliases = {len(operands): 0}
        operands.append(out)
        in_specs.append(hbm)
    count, height = len(shards), out_shape[0]
    rows, depth = sum(p.shape[0] for p in shards[0]), parts[0].shape[1]
    made = pl.pallas_call(
        functools.partial(
            column_kernel, bits, [(len(p), f) for p, f in zip(shards, own_first)], out is None
        ),
        in_specs=in_specs,
        out_specs=[hbm] + [vmem] * count,
        out_shape=[jax.ShapeDtypeStruct(out_shape, BF16)]
        + [jax.ShapeDtypeStruct((height, rows), BF16)] * count,
        scratch_shapes=[
            VMEM((count, rows, depth), BF16),
            VMEM((count, height, rows), BF16),
            pltpu.SemaphoreType.DMA((count,)),
        ],
        input_output_aliases=aliases,
        compiler_params=params(),
        cost_estimate=SMALL,
        name=name,
    )(*operands)
    return made[0], made[1:]


def put(source, out, spot, sem):
    width = source.shape[1]
    col = pl.multiple_of(spot * width, width)
    copy = pltpu.make_async_copy(source, out.at[:, pl.ds(col, width)], sem)
    copy.start()
    return copy


def place_kernel(bits, *refs):
    (*came, _, out, sems) = refs
    me = lax.axis_index("seq")
    copies = [put(ref, out, me ^ bit, sems.at[n]) for n, (bit, ref) in enumerate(zip(bits, came))]
    for copy in copies:
        copy.wait()


def place_columns(bits, came, out):
    vmem, hbm = pl.BlockSpec(memory_space=VMEM), pl.BlockSpec(memory_space=pltpu.HBM)
    return pl.pallas_call(
        functools.partial(place_kernel, bits),
        in_specs=[vmem] * len(came) + [hbm],
        out_specs=hbm,
        out_shape=jax.ShapeDtypeStruct(out.shape, BF16),
        scratch_shapes=[pltpu.SemaphoreType.DMA((len(came),))],
        input_output_aliases={len(came): 0},
        compiler_params=params(),
        cost_estimate=SMALL,
        name="place_columns",
    )(*came, out)


def swap(value, axis, size, bits):
    return lax.ppermute(value, axis, [(i, i ^ bits) for i in range(size)])


def by_exchange(
    size, hidden, token_ids, upstream, w_value, proj_in, proj_out, in_inverse, out_inverse, datastore
):
    ring = functools.partial(lambda bits, v: swap(v, "seq", size, bits))
    core, side = 1, 2
    far = [4 * k for k in range(1, size // 4)]
    cross = lambda v: swap(v, "grp", 2, 1)
    me, grp = lax.axis_index("seq"), lax.axis_index("grp")
    half = w_value.shape[0] // 2
    out_shape = (hidden.shape[0], w_value.shape[0] * size)
    own_half = lambda v: lax.dynamic_slice_in_dim(v, grp * half, half, 0)
    after = lambda v, *first: lax.optimization_barrier((v, *first))[0]

    with jax.named_scope("weight_first"):
        upstream_other, ids_other = ring(core, upstream), ring(core, token_ids)
        near = own_half(w_value)
        beside = ring(side, w_value)
        got = [ring(b, near if n else w_value) for n, b in enumerate(far)]
    masked, grad = query_gradient(
        token_ids, upstream, hidden, proj_in, proj_out, in_inverse, out_inverse
    )
    with jax.named_scope("weight_second"):
        h1, beside = after((got[0], beside), grad)
        y1 = [ring(side, h1[:half]), ring(side, h1[half:])]

    with jax.named_scope("query_exchange"):
        held, order, bit = after(grad, upstream_other)[None], [0], 4
        while bit < size:
            came = ring(bit, held)
            if bit == size // 2:
                held, came, rest, y1, beside = lax.optimization_barrier(
                    (held, came, got[1:], y1, beside)
                )
            held, order = join(held, came), order + [b ^ bit for b in order]
            bit *= 2
        came = ring(side, held)
        xs, ys = [cross(h) for h in rest], [ring(side, h) for h in rest[:-1]]
        came, xs, ys = lax.optimization_barrier((came, xs, ys))
        groups = [held, came, ring(core, held), ring(core, came)]
        order = [b ^ s for s in (0, side, core, side ^ core) for b in order]
    raw, power = raw_score_call(order, groups, datastore)

    with jax.named_scope("power"):
        for bits in ([core, side, core ^ side], far):
            parts = [ring(b, power) for b in bits]
            power = power + functools.reduce(jnp.add, parts)
        spread = jnp.sqrt(power[:, :1] / (datastore.shape[0] * size) + 1e-06)

    with jax.named_scope("weight_third"):
        ys.append(ring(side, rest[-1]))
        shards = {0: ((w_value,), False), side: ((beside,), False)}
        shards[far[0]], shards[far[0] ^ side] = ((h1,), False), (y1, False)
        for n, (b, h, x, y) in enumerate(zip(far[1:], rest, xs, ys)):
            d = ring(side, x) if n % 2 else cross(y)
            shards[b], shards[b ^ side] = ((h, x), True), ((y, d), True)

    with jax.named_scope("input_grad"):
        masked_other = mask(ids_other, upstream_other)
        out, came = None, []
        stages = [[0, far[0], side, far[0] ^ side], far[1:], [b ^ side for b in far[1:]]]
        for n, stage in enumerate(stages):
            out, away = columns(
                f"columns_{n}",
                stage,
                [masked, masked_other],
                [shards[b] for b in stage],
                out,
                out_shape,
            )
            came += [ring(core, a) for a in away]
        out = place_columns([core ^ b for stage in stages for b in stage], came, out)
    return out, raw / spread


def by_gather(
    size, hidden, token_ids, upstream, w_value, proj_in, proj_out, in_inverse, out_inverse, datastore
):
    queries, seq_tokens = token_ids.shape
    heads, head_dim, rank = proj_out.shape
    live_mask = (token_ids != 0).reshape(-1, 1).astype(BF16)
    masked = upstream * live_mask
    full_weight = lax.all_gather(w_value, "seq", axis=0, tiled=True)
    input_grad = lax.dot_general(masked, full_weight, LAST, preferred_element_type=F32).astype(BF16)
    left = jnp.dot(hidden, proj_in, preferred_element_type=F32).astype(BF16)
    right = jnp.einsum(
        "thd,hdr->thr", masked.reshape(-1, heads, head_dim), proj_out, preferred_element_type=F32
    ).astype(BF16)
    raw_grads = jnp.einsum(
        "qti,qthj->qhij",
        left.reshape(queries, seq_tokens, rank),
        right.reshape(queries, seq_tokens, heads, rank),
        preferred_element_type=F32,
    )
    half_way = jnp.einsum("hai,qhij->qhaj", in_inverse, raw_grads, precision=HIGHEST)
    pre = jnp.einsum("qhaj,hjb->qhab", half_way, out_inverse, precision=HIGHEST)
    grads = pre.astype(BF16).reshape(queries, -1)
    raw = lax.dot_general(
        lax.all_gather(grads, "seq", axis=0, tiled=True),
        datastore,
        LAST,
        preferred_element_type=F32,
    )
    power = lax.psum(jnp.sum(raw * raw, axis=1), "seq")
    spread = jnp.sqrt(power / (datastore.shape[0] * size) + 1e-06)
    return input_grad, raw / spread[:, None]


def solution(mesh):
    size, groups = mesh.shape["seq"], mesh.shape["grp"]

    def on_device(*args):
        hidden, token_ids, upstream, w_value = args[:4]
        fits = (
            groups == 2
            and size >= 8
            and size & (size - 1) == 0
            and token_ids.shape[0] == 1
            and w_value.shape[0] % 256 == 0
        )
        return (by_exchange if fits else by_gather)(size, *args)

    rows = P(("grp", "seq"), None)
    return jax.shard_map(
        on_device,
        mesh=mesh,
        in_specs=(rows, rows, rows, P("seq", None), P(), P(), P(), P(), rows),
        out_specs=(rows, P("grp", "seq")),
        check_vma=False,
    )
```

```python
import functools

import jax
import jax.numpy as jnp
from jax import lax
from jax.experimental import pallas as pl
from jax.experimental.pallas import tpu as pltpu
from jax.sharding import PartitionSpec as P

BF16 = jnp.bfloat16
F32 = jnp.float32
HIGHEST = lax.Precision.HIGHEST
LAST = (((1,), (1,)), ((), ()))
FIRST = (((0,), (0,)), ((), ()))
VMEM = pltpu.VMEM
MIB = 1024 * 1024


SMALL = pl.CostEstimate(flops=1, bytes_accessed=1, transcendentals=0)


def params(mib=24):
    return pltpu.CompilerParams(vmem_limit_bytes=mib * MIB)


def split(x):
    high = x.astype(BF16)
    return high, (x - high.astype(F32)).astype(BF16)


def mask_kernel(ids, up, masked):
    live = jnp.sum((ids[...] != 0).astype(jnp.int32))
    row = lax.broadcasted_iota(jnp.int32, up.shape, 0)
    masked[...] = jnp.where(row < live, up[...].astype(F32), 0.0).astype(BF16)


def mask(token_ids, upstream):
    return pl.pallas_call(
        mask_kernel,
        in_specs=[pl.BlockSpec(memory_space=VMEM)] * 2,
        out_specs=pl.BlockSpec(memory_space=VMEM),
        out_shape=jax.ShapeDtypeStruct(upstream.shape, BF16),
        compiler_params=params(),
        cost_estimate=SMALL,
        name="mask",
    )(token_ids, upstream)


def grad_kernel(ids, pout, a_inv, b_inv, up_hbm, hid_hbm, pin_hbm, masked, grad, up, hid, pin, sems):
    steps, _, chunk = hid.shape
    copies = [pltpu.make_async_copy(pin_hbm, pin, sems.at[0])]
    for k in range(steps):
        copies.append(
            pltpu.make_async_copy(hid_hbm.at[:, pl.ds(k * chunk, chunk)], hid.at[k], sems.at[1 + k])
        )
    copies.append(pltpu.make_async_copy(up_hbm, up, sems.at[1 + steps]))
    for copy in copies:
        copy.start()
    heads, rank, head_dim = pout.shape
    half = rank // 2
    out_sides, in_sides = [], []
    for h in range(heads):
        high, low = split(b_inv[h])
        side = lax.dot_general(pout[h], high, FIRST, preferred_element_type=F32)
        side += lax.dot_general(pout[h], low, FIRST, preferred_element_type=F32)
        high, low = split(side)
        out_sides.append(jnp.concatenate([high, low, high], axis=0))
        rows = [a_inv[h, pl.ds(odd, half, stride=2), :] for odd in range(2)]
        high, low = split(jnp.concatenate(rows, axis=0))
        in_sides.append(jnp.concatenate([high, high, low], axis=1))
    copies[0].wait()
    left = None
    for k in range(steps):
        copies[1 + k].wait()
        part = lax.dot_general(
            hid[k], pin[:, k * chunk : (k + 1) * chunk], LAST, preferred_element_type=F32
        )
        left = part if left is None else left + part
    copies[-1].wait()
    mask_kernel(ids, up, masked)
    both = jnp.dot(left.T.astype(BF16), masked[...], preferred_element_type=F32)
    high, low = split(both)
    for h in range(heads):
        lanes = slice(h * head_dim, (h + 1) * head_dim)
        terms = jnp.concatenate([high[:, lanes], high[:, lanes], low[:, lanes]], axis=1)
        mid = jnp.dot(terms, out_sides[h], preferred_element_type=F32)
        mid_high, mid_low = split(mid)
        terms = jnp.concatenate([mid_high, mid_low, mid_high], axis=0)
        pre = jnp.dot(in_sides[h], terms, preferred_element_type=F32)
        grad[0, h * half : (h + 1) * half, :] = jnp.concatenate(
            [pre[:half], pre[half:]], axis=1
        ).astype(BF16)


def query_gradient(token_ids, upstream, hidden, proj_in, proj_out, in_inverse, out_inverse):
    tokens, width = hidden.shape
    heads, head_dim, rank = proj_out.shape
    steps = 4 if width % 512 == 0 else 1
    vmem, hbm = pl.BlockSpec(memory_space=VMEM), pl.BlockSpec(memory_space=pltpu.HBM)
    whole = pl.BlockSpec()
    return pl.pallas_call(
        grad_kernel,
        in_specs=[whole] * 4 + [hbm] * 3,
        out_specs=[vmem, vmem],
        out_shape=[
            jax.ShapeDtypeStruct(upstream.shape, BF16),
            jax.ShapeDtypeStruct((1, heads * rank // 2, 2 * rank), BF16),
        ],
        scratch_shapes=[
            VMEM(upstream.shape, BF16),
            VMEM((steps, tokens, width // steps), BF16),
            VMEM((rank, width), BF16),
            pltpu.SemaphoreType.DMA((steps + 2,)),
        ],
        compiler_params=params(57),
        cost_estimate=SMALL,
        name="query_gradient",
    )(token_ids, proj_out.swapaxes(1, 2), in_inverse, out_inverse, upstream, hidden, proj_in.T)


def join_kernel(first, second, both):
    count = first.shape[0]
    both[:count] = first[...]
    both[count:] = second[...]


def join(first, second):
    vmem = pl.BlockSpec(memory_space=VMEM)
    shape = (first.shape[0] + second.shape[0], *first.shape[1:])
    return pl.pallas_call(
        join_kernel,
        in_specs=[vmem, vmem],
        out_specs=vmem,
        out_shape=jax.ShapeDtypeStruct(shape, first.dtype),
        compiler_params=params(),
        cost_estimate=SMALL,
        name="join",
    )(first, second)


def score_kernel(bits, *refs):
    *held, store_hbm, scores, power, wide, store, sems = refs
    steps, _, chunk = store.shape
    copies = []
    for k in range(steps):
        copies.append(
            pltpu.make_async_copy(store_hbm.at[:, pl.ds(k * chunk, chunk)], store.at[k], sems.at[k])
        )
        copies[-1].start()
    me = lax.axis_index("seq")
    queries = len(bits)
    groups, lanes = held[0].shape[1:]
    rows = [ref.at[k] for ref in held for k in range(ref.shape[0])]
    for bit, row in zip(bits, rows):
        wide[pl.ds(me ^ bit, groups, stride=queries), :] = row[...].astype(F32)
    total = jnp.zeros(scores.shape, F32)
    each = chunk // lanes
    for k in range(steps):
        lhs = jnp.concatenate(
            [
                wide[g * queries : (g + 1) * queries, :].astype(BF16)
                for g in range(k * each, (k + 1) * each)
            ],
            axis=1,
        )
        copies[k].wait()
        total += lax.dot_general(lhs, store[k], LAST, preferred_element_type=F32)
    scores[...] = total
    square = jnp.sum(total * total, axis=1, keepdims=True)
    power[...] = jnp.broadcast_to(square, power.shape)


def raw_score_call(bits, held, datastore):
    groups, lanes = held[0].shape[1:]
    queries, (rows, flat) = len(bits), datastore.shape
    steps = 4 if groups % 4 == 0 else 1
    vmem = pl.BlockSpec(memory_space=VMEM)
    return pl.pallas_call(
        functools.partial(score_kernel, bits),
        in_specs=[vmem] * len(held) + [pl.BlockSpec(memory_space=pltpu.HBM)],
        out_specs=[vmem, vmem],
        out_shape=[
            jax.ShapeDtypeStruct((queries, rows), F32),
            jax.ShapeDtypeStruct((queries, lanes), F32),
        ],
        scratch_shapes=[
            VMEM((groups * queries, lanes), F32),
            VMEM((steps, rows, flat // steps), BF16),
            pltpu.SemaphoreType.DMA((steps,)),
        ],
        compiler_params=params(48),
        cost_estimate=SMALL,
        name="raw_scores",
    )(*held, datastore)


def put(source, out, spot, sem):
    width = source.shape[1]
    col = pl.multiple_of(spot * width, width)
    copy = pltpu.make_async_copy(source, out.at[:, pl.ds(col, width)], sem)
    copy.start()
    return copy


def column_kernel(bits, pieces, fresh, mine, other, *refs):
    me, grp = lax.axis_index("seq"), lax.axis_index("grp")
    shard_refs = []
    for count, _ in pieces:
        shard_refs.append(refs[:count])
        refs = refs[count:]
    out, *away, weight, tile, sems = refs[0 if fresh else 1 :]
    copies = []
    for k, (bit, parts) in enumerate(zip(bits, shard_refs)):
        if len(parts) == 1:
            (whole,) = parts
        else:
            whole = weight.at[k]
            rows = parts[0].shape[0]
            for part, half in zip(parts, (grp, 1 - grp) if pieces[k][1] else (0, 1)):
                whole[pl.ds(pl.multiple_of(half * rows, rows), rows), :] = part[...]
        tile[k] = lax.dot_general(mine[...], whole[...], LAST, preferred_element_type=F32).astype(BF16)
        copies.append(put(tile.at[k], out, me ^ bit, sems.at[k]))
        away[k][...] = lax.dot_general(
            other[...], whole[...], LAST, preferred_element_type=F32
        ).astype(BF16)
    for copy in copies:
        copy.wait()


def columns(name, bits, tokens, shards, out, out_shape):
    vmem, hbm = pl.BlockSpec(memory_space=VMEM), pl.BlockSpec(memory_space=pltpu.HBM)
    shards, own_first = [s[0] for s in shards], [s[1] for s in shards]
    parts = [p for shard in shards for p in shard]
    operands = [*tokens, *parts]
    in_specs = [vmem] * len(operands)
    aliases = {}
    if out is not None:
        aliases = {len(operands): 0}
        operands.append(out)
        in_specs.append(hbm)
    count, height = len(shards), out_shape[0]
    rows, depth = sum(p.shape[0] for p in shards[0]), parts[0].shape[1]
    made = pl.pallas_call(
        functools.partial(
            column_kernel, bits, [(len(p), f) for p, f in zip(shards, own_first)], out is None
        ),
        in_specs=in_specs,
        out_specs=[hbm] + [vmem] * count,
        out_shape=[jax.ShapeDtypeStruct(out_shape, BF16)]
        + [jax.ShapeDtypeStruct((height, rows), BF16)] * count,
        scratch_shapes=[
            VMEM((count, rows, depth), BF16),
            VMEM((count, height, rows), BF16),
            pltpu.SemaphoreType.DMA((count,)),
        ],
        input_output_aliases=aliases,
        compiler_params=params(),
        cost_estimate=SMALL,
        name=name,
    )(*operands)
    return made[0], made[1:]


def put(source, out, spot, sem):
    width = source.shape[1]
    col = pl.multiple_of(spot * width, width)
    copy = pltpu.make_async_copy(source, out.at[:, pl.ds(col, width)], sem)
    copy.start()
    return copy


def place_kernel(bits, *refs):
    (*came, _, out, sems) = refs
    me = lax.axis_index("seq")
    copies = [put(ref, out, me ^ bit, sems.at[n]) for n, (bit, ref) in enumerate(zip(bits, came))]
    for copy in copies:
        copy.wait()


def place_columns(bits, came, out):
    vmem, hbm = pl.BlockSpec(memory_space=VMEM), pl.BlockSpec(memory_space=pltpu.HBM)
    return pl.pallas_call(
        functools.partial(place_kernel, bits),
        in_specs=[vmem] * len(came) + [hbm],
        out_specs=hbm,
        out_shape=jax.ShapeDtypeStruct(out.shape, BF16),
        scratch_shapes=[pltpu.SemaphoreType.DMA((len(came),))],
        input_output_aliases={len(came): 0},
        compiler_params=params(),
        cost_estimate=SMALL,
        name="place_columns",
    )(*came, out)


def swap(value, axis, size, bits):
    return lax.ppermute(value, axis, [(i, i ^ bits) for i in range(size)])


def by_exchange(
    size, hidden, token_ids, upstream, w_value, proj_in, proj_out, in_inverse, out_inverse, datastore
):
    ring = functools.partial(lambda bits, v: swap(v, "seq", size, bits))
    core, side = 1, 2
    far = [4 * k for k in range(1, size // 4)]
    cross = lambda v: swap(v, "grp", 2, 1)
    me, grp = lax.axis_index("seq"), lax.axis_index("grp")
    half = w_value.shape[0] // 2
    out_shape = (hidden.shape[0], w_value.shape[0] * size)
    own_half = lambda v: lax.dynamic_slice_in_dim(v, grp * half, half, 0)
    after = lambda v, *first: lax.optimization_barrier((v, *first))[0]

    with jax.named_scope("weight_first"):
        upstream_other, ids_other = ring(core, upstream), ring(core, token_ids)
        near = own_half(w_value)
        beside = ring(side, w_value)
        got = [ring(b, near) for b in far]
    masked, grad = query_gradient(
        token_ids, upstream, hidden, proj_in, proj_out, in_inverse, out_inverse
    )
    with jax.named_scope("weight_second"):
        h1, beside = after((got[0], beside), grad)
        x1, y1 = cross(h1), ring(side, h1)

    with jax.named_scope("query_exchange"):
        held, order, bit = after(grad, upstream_other), [0], side
        while bit < size // 2:
            came = ring(bit, held)
            if bit == size // 4:
                held, came, rest, x1, y1, beside = lax.optimization_barrier(
                    (held, came, got[1:], x1, y1, beside)
                )
            held, order = join(held, came), order + [b ^ bit for b in order]
            bit *= 2
        came = ring(bit, held)
        xs, ys = [cross(h) for h in rest], [ring(side, h) for h in rest]
        came, xs, ys = lax.optimization_barrier((came, xs, ys))
        groups = [held, came, ring(core, held), ring(core, came)]
        order = [b ^ s for s in (0, bit, core, bit ^ core) for b in order]
    raw, power = raw_score_call(order, groups, datastore)

    with jax.named_scope("weight_third"):
        ds = [ring(side, x) if n % 2 else cross(y) for n, (x, y) in enumerate(zip(xs, ys))]
        d1 = cross(y1)

    shards = {0: ((w_value,), False), side: ((beside,), False), far[0]: ((h1, x1), True)}
    for b, h, x in zip(far[1:], rest, xs):
        shards[b] = (h, x), True
    out, came = None, []
    tokens = [masked, mask(ids_other, upstream_other)]

    def stage_columns(n, stage, out):
        out, away = columns(f"columns_{n}", stage, tokens, [shards[b] for b in stage], out, out_shape)
        return out, [ring(core, a) for a in away]

    stages = [[0, side] + far, [b ^ side for b in far]]
    with jax.named_scope("input_grad"):
        out, came = stage_columns(0, stages[0], None)

    with jax.named_scope("power"):
        for n, bits in enumerate(([core, side, core ^ side], far)):
            parts = [ring(b, power) for b in bits]
            power = power + functools.reduce(jnp.add, parts)
            if n == 0:
                power, ds, d1, out = lax.optimization_barrier((power, ds, d1, out))
        spread = jnp.sqrt(power[:, :1] / (datastore.shape[0] * size) + 1e-06)

    shards[far[0] ^ side] = (y1, d1), True
    for b, y, d in zip(far[1:], ys, ds):
        shards[b ^ side] = (y, d), True
    with jax.named_scope("input_grad"):
        out, last = stage_columns(1, stages[1], out)
        out = place_columns([core ^ b for stage in stages for b in stage], [*came, *last], out)
    return out, raw / spread


def by_gather(
    size, hidden, token_ids, upstream, w_value, proj_in, proj_out, in_inverse, out_inverse, datastore
):
    queries, seq_tokens = token_ids.shape
    heads, head_dim, rank = proj_out.shape
    live_mask = (token_ids != 0).reshape(-1, 1).astype(BF16)
    masked = upstream * live_mask
    full_weight = lax.all_gather(w_value, "seq", axis=0, tiled=True)
    input_grad = lax.dot_general(masked, full_weight, LAST, preferred_element_type=F32).astype(BF16)
    left = jnp.dot(hidden, proj_in, preferred_element_type=F32).astype(BF16)
    right = jnp.einsum(
        "thd,hdr->thr", masked.reshape(-1, heads, head_dim), proj_out, preferred_element_type=F32
    ).astype(BF16)
    raw_grads = jnp.einsum(
        "qti,qthj->qhij",
        left.reshape(queries, seq_tokens, rank),
        right.reshape(queries, seq_tokens, heads, rank),
        preferred_element_type=F32,
    )
    half_way = jnp.einsum("hai,qhij->qhaj", in_inverse, raw_grads, precision=HIGHEST)
    pre = jnp.einsum("qhaj,hjb->qhab", half_way, out_inverse, precision=HIGHEST)
    grads = pre.astype(BF16).reshape(queries, -1)
    raw = lax.dot_general(
        lax.all_gather(grads, "seq", axis=0, tiled=True),
        datastore,
        LAST,
        preferred_element_type=F32,
    )
    power = lax.psum(jnp.sum(raw * raw, axis=1), "seq")
    spread = jnp.sqrt(power / (datastore.shape[0] * size) + 1e-06)
    return input_grad, raw / spread[:, None]


def solution(mesh):
    size, groups = mesh.shape["seq"], mesh.shape["grp"]

    def on_device(*args):
        hidden, token_ids, upstream, w_value = args[:4]
        fits = (
            groups == 2
            and size >= 8
            and size & (size - 1) == 0
            and token_ids.shape[0] == 1
            and w_value.shape[0] % 256 == 0
        )
        return (by_exchange if fits else by_gather)(size, *args)

    rows = P(("grp", "seq"), None)
    return jax.shard_map(
        on_device,
        mesh=mesh,
        in_specs=(rows, rows, rows, P("seq", None), P(), P(), P(), P(), rows),
        out_specs=(rows, P("grp", "seq")),
        check_vma=False,
    )
```

```python
import functools

import jax
import jax.numpy as jnp
from jax import lax
from jax.experimental import pallas as pl
from jax.experimental.pallas import tpu as pltpu
from jax.sharding import PartitionSpec as P

BF16 = jnp.bfloat16
F32 = jnp.float32
HIGHEST = lax.Precision.HIGHEST
LAST = (((1,), (1,)), ((), ()))
FIRST = (((0,), (0,)), ((), ()))
VMEM = pltpu.VMEM
MIB = 1024 * 1024


SMALL = pl.CostEstimate(flops=1, bytes_accessed=1, transcendentals=0)


def params(mib=24):
    return pltpu.CompilerParams(vmem_limit_bytes=mib * MIB)


def split(x):
    high = x.astype(BF16)
    return high, (x - high.astype(F32)).astype(BF16)


def mask_kernel(ids, up, masked):
    live = jnp.sum((ids[...] != 0).astype(jnp.int32))
    row = lax.broadcasted_iota(jnp.int32, up.shape, 0)
    masked[...] = jnp.where(row < live, up[...].astype(F32), 0.0).astype(BF16)


def grad_kernel(ids, pout, a_inv, b_inv, up_hbm, hid_hbm, pin_hbm, masked, grad, up, hid, pin, sems):
    steps, _, chunk = hid.shape
    copies = [pltpu.make_async_copy(pin_hbm, pin, sems.at[0])]
    for k in range(steps):
        copies.append(
            pltpu.make_async_copy(hid_hbm.at[:, pl.ds(k * chunk, chunk)], hid.at[k], sems.at[1 + k])
        )
    copies.append(pltpu.make_async_copy(up_hbm, up, sems.at[1 + steps]))
    for copy in copies:
        copy.start()
    heads, rank, head_dim = pout.shape
    half = rank // 2
    out_sides, in_sides = [], []
    for h in range(heads):
        high, low = split(b_inv[h])
        side = lax.dot_general(pout[h], high, FIRST, preferred_element_type=F32)
        side += lax.dot_general(pout[h], low, FIRST, preferred_element_type=F32)
        high, low = split(side)
        out_sides.append(jnp.concatenate([high, low, high], axis=0))
        rows = [a_inv[h, pl.ds(odd, half, stride=2), :] for odd in range(2)]
        high, low = split(jnp.concatenate(rows, axis=0))
        in_sides.append(jnp.concatenate([high, high, low], axis=1))
    copies[0].wait()
    left = None
    for k in range(steps):
        copies[1 + k].wait()
        part = lax.dot_general(
            hid[k], pin[:, k * chunk : (k + 1) * chunk], LAST, preferred_element_type=F32
        )
        left = part if left is None else left + part
    copies[-1].wait()
    mask_kernel(ids, up, masked)
    both = jnp.dot(left.T.astype(BF16), masked[...], preferred_element_type=F32)
    high, low = split(both)
    for h in range(heads):
        lanes = slice(h * head_dim, (h + 1) * head_dim)
        terms = jnp.concatenate([high[:, lanes], high[:, lanes], low[:, lanes]], axis=1)
        mid = jnp.dot(terms, out_sides[h], preferred_element_type=F32)
        mid_high, mid_low = split(mid)
        terms = jnp.concatenate([mid_high, mid_low, mid_high], axis=0)
        pre = jnp.dot(in_sides[h], terms, preferred_element_type=F32)
        grad[0, h * half : (h + 1) * half, :] = jnp.concatenate(
            [pre[:half], pre[half:]], axis=1
        ).astype(BF16)


def query_gradient(token_ids, upstream, hidden, proj_in, proj_out, in_inverse, out_inverse):
    tokens, width = hidden.shape
    heads, head_dim, rank = proj_out.shape
    steps = 4 if width % 512 == 0 else 1
    vmem, hbm = pl.BlockSpec(memory_space=VMEM), pl.BlockSpec(memory_space=pltpu.HBM)
    whole = pl.BlockSpec()
    return pl.pallas_call(
        grad_kernel,
        in_specs=[whole] * 4 + [hbm] * 3,
        out_specs=[vmem, vmem],
        out_shape=[
            jax.ShapeDtypeStruct(upstream.shape, BF16),
            jax.ShapeDtypeStruct((1, heads * rank // 2, 2 * rank), BF16),
        ],
        scratch_shapes=[
            VMEM(upstream.shape, BF16),
            VMEM((steps, tokens, width // steps), BF16),
            VMEM((rank, width), BF16),
            pltpu.SemaphoreType.DMA((steps + 2,)),
        ],
        compiler_params=params(57),
        cost_estimate=SMALL,
        name="query_gradient",
    )(token_ids, proj_out.swapaxes(1, 2), in_inverse, out_inverse, upstream, hidden, proj_in.T)


def join_kernel(first, second, both):
    count = first.shape[0]
    both[:count] = first[...]
    both[count:] = second[...]


def join(first, second):
    vmem = pl.BlockSpec(memory_space=VMEM)
    shape = (first.shape[0] + second.shape[0], *first.shape[1:])
    return pl.pallas_call(
        join_kernel,
        in_specs=[vmem, vmem],
        out_specs=vmem,
        out_shape=jax.ShapeDtypeStruct(shape, first.dtype),
        compiler_params=params(),
        cost_estimate=SMALL,
        name="join",
    )(first, second)


def score_kernel(bits, *refs):
    *held, store_hbm, scores, power, wide, store, sems = refs
    steps, _, chunk = store.shape
    copies = []
    for k in range(steps):
        copies.append(
            pltpu.make_async_copy(store_hbm.at[:, pl.ds(k * chunk, chunk)], store.at[k], sems.at[k])
        )
        copies[-1].start()
    me = lax.axis_index("seq")
    queries = len(bits)
    groups, lanes = held[0].shape[1:]
    rows = [ref.at[k] for ref in held for k in range(ref.shape[0])]
    for bit, row in zip(bits, rows):
        wide[pl.ds(me ^ bit, groups, stride=queries), :] = row[...].astype(F32)
    total = jnp.zeros(scores.shape, F32)
    each = chunk // lanes
    for k in range(steps):
        lhs = jnp.concatenate(
            [
                wide[g * queries : (g + 1) * queries, :].astype(BF16)
                for g in range(k * each, (k + 1) * each)
            ],
            axis=1,
        )
        copies[k].wait()
        total += lax.dot_general(lhs, store[k], LAST, preferred_element_type=F32)
    scores[...] = total
    square = jnp.sum(total * total, axis=1, keepdims=True)
    power[...] = jnp.broadcast_to(square, power.shape)


def raw_score_call(bits, held, datastore):
    groups, lanes = held[0].shape[1:]
    queries, (rows, flat) = len(bits), datastore.shape
    steps = 4 if groups % 4 == 0 else 1
    vmem = pl.BlockSpec(memory_space=VMEM)
    return pl.pallas_call(
        functools.partial(score_kernel, bits),
        in_specs=[vmem] * len(held) + [pl.BlockSpec(memory_space=pltpu.HBM)],
        out_specs=[vmem, vmem],
        out_shape=[
            jax.ShapeDtypeStruct((queries, rows), F32),
            jax.ShapeDtypeStruct((queries, lanes), F32),
        ],
        scratch_shapes=[
            VMEM((groups * queries, lanes), F32),
            VMEM((steps, rows, flat // steps), BF16),
            pltpu.SemaphoreType.DMA((steps,)),
        ],
        compiler_params=params(48),
        cost_estimate=SMALL,
        name="raw_scores",
    )(*held, datastore)


def put(source, out, spot, sem):
    width = source.shape[1]
    col = pl.multiple_of(spot * width, width)
    copy = pltpu.make_async_copy(source, out.at[:, pl.ds(col, width)], sem)
    copy.start()
    return copy


def column_kernel(bits, pieces, fresh, mine, other, *refs):
    me, grp = lax.axis_index("seq"), lax.axis_index("grp")
    shard_refs = []
    for spots, _ in pieces:
        shard_refs.append([ref if at is None else ref.at[at] for at, ref in zip(spots, refs)])
        refs = refs[len(spots) :]
    out, away, weight, tile, sems = refs[0 if fresh else 1 :]
    copies = []
    for k, (bit, parts) in enumerate(zip(bits, shard_refs)):
        if len(parts) == 1:
            (whole,) = parts
        else:
            whole = weight.at[k]
            rows = parts[0].shape[0]
            for part, half in zip(parts, (grp, 1 - grp) if pieces[k][1] else (0, 1)):
                whole[pl.ds(pl.multiple_of(half * rows, rows), rows), :] = part[...]
        tile[k] = lax.dot_general(mine[...], whole[...], LAST, preferred_element_type=F32).astype(BF16)
        copies.append(put(tile.at[k], out, me ^ bit, sems.at[k]))
        away[k] = lax.dot_general(
            other[...], whole[...], LAST, preferred_element_type=F32
        ).astype(BF16)
    for copy in copies:
        copy.wait()


def columns(name, bits, tokens, shards, out, out_shape):
    vmem, hbm = pl.BlockSpec(memory_space=VMEM), pl.BlockSpec(memory_space=pltpu.HBM)
    split_parts = [[p if isinstance(p, tuple) else (p, None) for p in shard[0]] for shard in shards]
    pieces = [([at for _, at in parts], shard[1]) for parts, shard in zip(split_parts, shards)]
    operands = [*tokens, *(array for parts in split_parts for array, _ in parts)]
    in_specs = [vmem] * len(operands)
    aliases = {}
    if out is not None:
        aliases = {len(operands): 0}
        operands.append(out)
        in_specs.append(hbm)
    count, height = len(shards), out_shape[0]
    rows, depth = sum(array.shape[-2] for array, _ in split_parts[0]), tokens[0].shape[1]
    return pl.pallas_call(
        functools.partial(column_kernel, bits, pieces, out is None),
        in_specs=in_specs,
        out_specs=[hbm, vmem],
        out_shape=[
            jax.ShapeDtypeStruct(out_shape, BF16),
            jax.ShapeDtypeStruct((count, height, rows), BF16),
        ],
        scratch_shapes=[
            VMEM((count, rows, depth), BF16),
            VMEM((count, height, rows), BF16),
            pltpu.SemaphoreType.DMA((count,)),
        ],
        input_output_aliases=aliases,
        compiler_params=params(),
        cost_estimate=SMALL,
        name=name,
    )(*operands)


def put(source, out, spot, sem):
    width = source.shape[1]
    col = pl.multiple_of(spot * width, width)
    copy = pltpu.make_async_copy(source, out.at[:, pl.ds(col, width)], sem)
    copy.start()
    return copy


def place_kernel(bits, ids, *refs):
    (*came, _, out, tiles, sems) = refs
    me = lax.axis_index("seq")
    live = jnp.sum((ids[...] != 0).astype(jnp.int32))
    row = lax.broadcasted_iota(jnp.int32, tiles.shape[1:], 0)
    copies = []
    given = [ref.at[k] for ref in came for k in range(ref.shape[0])]
    for n, (bit, ref) in enumerate(zip(bits, given)):
        tiles[n] = jnp.where(row < live, ref[...].astype(F32), 0.0).astype(BF16)
        copies.append(put(tiles.at[n], out, me ^ bit, sems.at[n]))
    for copy in copies:
        copy.wait()


def place_columns(bits, token_ids, came, out):
    vmem, hbm = pl.BlockSpec(memory_space=VMEM), pl.BlockSpec(memory_space=pltpu.HBM)
    return pl.pallas_call(
        functools.partial(place_kernel, bits),
        in_specs=[vmem] * (1 + len(came)) + [hbm],
        out_specs=hbm,
        out_shape=jax.ShapeDtypeStruct(out.shape, BF16),
        scratch_shapes=[
            VMEM((len(bits), *came[0].shape[1:]), BF16),
            pltpu.SemaphoreType.DMA((len(bits),)),
        ],
        input_output_aliases={1 + len(came): 0},
        compiler_params=params(),
        cost_estimate=SMALL,
        name="place_columns",
    )(token_ids, *came, out)


def swap(value, axis, size, bits):
    return lax.ppermute(value, axis, [(i, i ^ bits) for i in range(size)])


def by_exchange(
    size, hidden, token_ids, upstream, w_value, proj_in, proj_out, in_inverse, out_inverse, datastore
):
    ring = functools.partial(lambda bits, v: swap(v, "seq", size, bits))
    core, side = 1, 2
    far = [4 * k for k in range(1, size // 4)]
    cross = lambda v: swap(v, "grp", 2, 1)
    me, grp = lax.axis_index("seq"), lax.axis_index("grp")
    half = w_value.shape[0] // 2
    out_shape = (hidden.shape[0], w_value.shape[0] * size)
    own_half = lambda v: lax.dynamic_slice_in_dim(v, grp * half, half, 0)
    after = lambda v, *first: lax.optimization_barrier((v, *first))[0]

    with jax.named_scope("weight_first"):
        upstream_other = ring(core, upstream)
        near = own_half(w_value)
        beside = ring(side, w_value)
        got = [ring(b, near) for b in far]
    masked, grad = query_gradient(
        token_ids, upstream, hidden, proj_in, proj_out, in_inverse, out_inverse
    )
    stages = [[0, side, far[0]], far[1:], [b ^ side for b in far]]

    def stage_columns(n, out):
        with jax.named_scope("input_grad"):
            tokens, each = [masked, upstream_other], [shards[b] for b in stages[n]]
            out, away = columns(f"columns_{n}", stages[n], tokens, each, out, out_shape)
            return out, ring(core, away)

    with jax.named_scope("weight_second"):
        h1, beside = after((got[0], beside), grad)
        x1, y1 = cross(h1), ring(side, h1)

    with jax.named_scope("query_exchange"):
        held, order, bit = after(grad, upstream_other), [0], side
        while bit < size // 2:
            came = ring(bit, held)
            if bit == size // 4:
                held, came, rest, x1, y1, beside = lax.optimization_barrier(
                    (held, came, got[1:], x1, y1, beside)
                )
            held, order = join(held, came), order + [b ^ bit for b in order]
            bit *= 2
        shards = {0: ((w_value,), False), side: ((beside,), False), far[0]: ((h1, x1), True)}
        out, back = stage_columns(0, None)
        came_back = [back]
        came = ring(bit, held)
        xs, ys = [cross(h) for h in rest], [ring(side, h) for h in rest]
        came, xs, ys, out = lax.optimization_barrier((came, xs, ys, out))
        groups = [held, came, ring(core, held), ring(core, came)]
        order = [b ^ s for s in (0, bit, core, bit ^ core) for b in order]
    raw, power = raw_score_call(order, groups, datastore)

    with jax.named_scope("weight_third"):
        d3 = ring(side, xs[-1])
        pair = cross(join(y1[None], ys[0][None]))
        for b, h, x in zip(far[1:], rest, xs):
            shards[b] = (h, x), True
        out, back = stage_columns(1, after(out, power))
        came_back.append(back)

    with jax.named_scope("power"):
        for bits in ([core], [side], far):
            parts = [ring(b, power) for b in bits]
            if bits == [side]:
                power, parts, out = lax.optimization_barrier((power, parts, out))
            if bits is far:
                power, parts, d3, pair, out = lax.optimization_barrier((power, parts, d3, pair, out))
            power = power + functools.reduce(jnp.add, parts)
        spread = jnp.sqrt(power[:, :1] / (datastore.shape[0] * size) + 1e-06)

    shards[far[0] ^ side] = (y1, (pair, 0)), True
    shards[far[1] ^ side] = (ys[0], (pair, 1)), True
    shards[far[2] ^ side] = (ys[1], d3), True
    out, back = stage_columns(2, out)
    came_back.append(back)
    out = place_columns([core ^ b for stage in stages for b in stage], token_ids, came_back, out)
    return out, raw / spread


def by_gather(
    size, hidden, token_ids, upstream, w_value, proj_in, proj_out, in_inverse, out_inverse, datastore
):
    queries, seq_tokens = token_ids.shape
    heads, head_dim, rank = proj_out.shape
    live_mask = (token_ids != 0).reshape(-1, 1).astype(BF16)
    masked = upstream * live_mask
    full_weight = lax.all_gather(w_value, "seq", axis=0, tiled=True)
    input_grad = lax.dot_general(masked, full_weight, LAST, preferred_element_type=F32).astype(BF16)
    left = jnp.dot(hidden, proj_in, preferred_element_type=F32).astype(BF16)
    right = jnp.einsum(
        "thd,hdr->thr", masked.reshape(-1, heads, head_dim), proj_out, preferred_element_type=F32
    ).astype(BF16)
    raw_grads = jnp.einsum(
        "qti,qthj->qhij",
        left.reshape(queries, seq_tokens, rank),
        right.reshape(queries, seq_tokens, heads, rank),
        preferred_element_type=F32,
    )
    half_way = jnp.einsum("hai,qhij->qhaj", in_inverse, raw_grads, precision=HIGHEST)
    pre = jnp.einsum("qhaj,hjb->qhab", half_way, out_inverse, precision=HIGHEST)
    grads = pre.astype(BF16).reshape(queries, -1)
    raw = lax.dot_general(
        lax.all_gather(grads, "seq", axis=0, tiled=True),
        datastore,
        LAST,
        preferred_element_type=F32,
    )
    power = lax.psum(jnp.sum(raw * raw, axis=1), "seq")
    spread = jnp.sqrt(power / (datastore.shape[0] * size) + 1e-06)
    return input_grad, raw / spread[:, None]


def solution(mesh):
    size, groups = mesh.shape["seq"], mesh.shape["grp"]

    def on_device(*args):
        hidden, token_ids, upstream, w_value = args[:4]
        fits = (
            groups == 2
            and size == 16
            and token_ids.shape[0] == 1
            and w_value.shape[0] % 256 == 0
        )
        return (by_exchange if fits else by_gather)(size, *args)

    rows = P(("grp", "seq"), None)
    return jax.shard_map(
        on_device,
        mesh=mesh,
        in_specs=(rows, rows, rows, P("seq", None), P(), P(), P(), P(), rows),
        out_specs=(rows, P("grp", "seq")),
        check_vma=False,
    )
```

```python
import functools

import jax
import jax.numpy as jnp
from jax import lax
from jax.experimental import pallas as pl
from jax.experimental.pallas import tpu as pltpu
from jax.sharding import PartitionSpec as P

BF16 = jnp.bfloat16
F32 = jnp.float32
HIGHEST = lax.Precision.HIGHEST
LAST = (((1,), (1,)), ((), ()))
FIRST = (((0,), (0,)), ((), ()))
VMEM = pltpu.VMEM
MIB = 1024 * 1024


SMALL = pl.CostEstimate(flops=1, bytes_accessed=1, transcendentals=0)


def params(mib=24):
    return pltpu.CompilerParams(vmem_limit_bytes=mib * MIB)


def split(x):
    high = x.astype(BF16)
    return high, (x - high.astype(F32)).astype(BF16)


def mask_kernel(ids, up, masked):
    live = jnp.sum((ids[...] != 0).astype(jnp.int32))
    row = lax.broadcasted_iota(jnp.int32, up.shape, 0)
    masked[...] = jnp.where(row < live, up[...].astype(F32), 0.0).astype(BF16)


def grad_kernel(ids, pout, a_inv, b_inv, up_hbm, hid_hbm, pin_hbm, masked, grad, up, hid, pin, sems):
    steps, _, chunk = hid.shape
    copies = [pltpu.make_async_copy(pin_hbm, pin, sems.at[0])]
    for k in range(steps):
        copies.append(
            pltpu.make_async_copy(hid_hbm.at[:, pl.ds(k * chunk, chunk)], hid.at[k], sems.at[1 + k])
        )
    copies.append(pltpu.make_async_copy(up_hbm, up, sems.at[1 + steps]))
    for copy in copies:
        copy.start()
    heads, rank, head_dim = pout.shape
    half = rank // 2
    out_sides, in_sides = [], []
    for h in range(heads):
        high, low = split(b_inv[h])
        side = lax.dot_general(pout[h], high, FIRST, preferred_element_type=F32)
        side += lax.dot_general(pout[h], low, FIRST, preferred_element_type=F32)
        high, low = split(side)
        out_sides.append(jnp.concatenate([high, low, high], axis=0))
        rows = [a_inv[h, pl.ds(odd, half, stride=2), :] for odd in range(2)]
        high, low = split(jnp.concatenate(rows, axis=0))
        in_sides.append(jnp.concatenate([high, high, low], axis=1))
    copies[0].wait()
    left = None
    for k in range(steps):
        copies[1 + k].wait()
        part = lax.dot_general(
            hid[k], pin[:, k * chunk : (k + 1) * chunk], LAST, preferred_element_type=F32
        )
        left = part if left is None else left + part
    copies[-1].wait()
    mask_kernel(ids, up, masked)
    both = jnp.dot(left.T.astype(BF16), masked[...], preferred_element_type=F32)
    high, low = split(both)
    for h in range(heads):
        lanes = slice(h * head_dim, (h + 1) * head_dim)
        terms = jnp.concatenate([high[:, lanes], high[:, lanes], low[:, lanes]], axis=1)
        mid = jnp.dot(terms, out_sides[h], preferred_element_type=F32)
        mid_high, mid_low = split(mid)
        terms = jnp.concatenate([mid_high, mid_low, mid_high], axis=0)
        pre = jnp.dot(in_sides[h], terms, preferred_element_type=F32)
        grad[0, h * half : (h + 1) * half, :] = jnp.concatenate(
            [pre[:half], pre[half:]], axis=1
        ).astype(BF16)


def query_gradient(token_ids, upstream, hidden, proj_in, proj_out, in_inverse, out_inverse):
    tokens, width = hidden.shape
    heads, head_dim, rank = proj_out.shape
    steps = 4 if width % 512 == 0 else 1
    vmem, hbm = pl.BlockSpec(memory_space=VMEM), pl.BlockSpec(memory_space=pltpu.HBM)
    whole = pl.BlockSpec()
    return pl.pallas_call(
        grad_kernel,
        in_specs=[whole] * 4 + [hbm] * 3,
        out_specs=[vmem, vmem],
        out_shape=[
            jax.ShapeDtypeStruct(upstream.shape, BF16),
            jax.ShapeDtypeStruct((1, heads * rank // 2, 2 * rank), BF16),
        ],
        scratch_shapes=[
            VMEM(upstream.shape, BF16),
            VMEM((steps, tokens, width // steps), BF16),
            VMEM((rank, width), BF16),
            pltpu.SemaphoreType.DMA((steps + 2,)),
        ],
        compiler_params=params(57),
        cost_estimate=SMALL,
        name="query_gradient",
    )(token_ids, proj_out.swapaxes(1, 2), in_inverse, out_inverse, upstream, hidden, proj_in.T)


def join_kernel(first, second, both):
    count = first.shape[0]
    both[:count] = first[...]
    both[count:] = second[...]


def join(first, second):
    vmem = pl.BlockSpec(memory_space=VMEM)
    shape = (first.shape[0] + second.shape[0], *first.shape[1:])
    return pl.pallas_call(
        join_kernel,
        in_specs=[vmem, vmem],
        out_specs=vmem,
        out_shape=jax.ShapeDtypeStruct(shape, first.dtype),
        compiler_params=params(),
        cost_estimate=SMALL,
        name="join",
    )(first, second)


def pair_kernel(spots, first, second, both):
    for n, (at, ref) in enumerate(zip(spots, (first, second))):
        both[n] = ref[...] if at is None else ref[at]


def pair_up(first, second):
    given = [p if isinstance(p, tuple) else (p, None) for p in (first, second)]
    vmem = pl.BlockSpec(memory_space=VMEM)
    shape = (2, *given[0][0].shape[-2:])
    return pl.pallas_call(
        functools.partial(pair_kernel, [at for _, at in given]),
        in_specs=[vmem, vmem],
        out_specs=vmem,
        out_shape=jax.ShapeDtypeStruct(shape, given[0][0].dtype),
        compiler_params=params(),
        cost_estimate=SMALL,
        name="pair_up",
    )(*(array for array, _ in given))


def score_kernel(bits, *refs):
    *held, store_hbm, scores, power, wide, store, sems = refs
    steps, _, chunk = store.shape
    copies = []
    for k in range(steps):
        copies.append(
            pltpu.make_async_copy(store_hbm.at[:, pl.ds(k * chunk, chunk)], store.at[k], sems.at[k])
        )
        copies[-1].start()
    me = lax.axis_index("seq")
    queries = len(bits)
    groups, lanes = held[0].shape[1:]
    rows = [ref.at[k] for ref in held for k in range(ref.shape[0])]
    for bit, row in zip(bits, rows):
        wide[pl.ds(me ^ bit, groups, stride=queries), :] = row[...].astype(F32)
    total = jnp.zeros(scores.shape, F32)
    each = chunk // lanes
    for k in range(steps):
        lhs = jnp.concatenate(
            [
                wide[g * queries : (g + 1) * queries, :].astype(BF16)
                for g in range(k * each, (k + 1) * each)
            ],
            axis=1,
        )
        copies[k].wait()
        total += lax.dot_general(lhs, store[k], LAST, preferred_element_type=F32)
    scores[...] = total
    square = jnp.sum(total * total, axis=1, keepdims=True)
    power[...] = jnp.broadcast_to(square, power.shape)


def raw_score_call(bits, held, datastore):
    groups, lanes = held[0].shape[1:]
    queries, (rows, flat) = len(bits), datastore.shape
    steps = 4 if groups % 4 == 0 else 1
    vmem = pl.BlockSpec(memory_space=VMEM)
    return pl.pallas_call(
        functools.partial(score_kernel, bits),
        in_specs=[vmem] * len(held) + [pl.BlockSpec(memory_space=pltpu.HBM)],
        out_specs=[vmem, vmem],
        out_shape=[
            jax.ShapeDtypeStruct((queries, rows), F32),
            jax.ShapeDtypeStruct((queries, lanes), F32),
        ],
        scratch_shapes=[
            VMEM((groups * queries, lanes), F32),
            VMEM((steps, rows, flat // steps), BF16),
            pltpu.SemaphoreType.DMA((steps,)),
        ],
        compiler_params=params(48),
        cost_estimate=SMALL,
        name="raw_scores",
    )(*held, datastore)


def put(source, out, spot, sem):
    width = source.shape[1]
    col = pl.multiple_of(spot * width, width)
    copy = pltpu.make_async_copy(source, out.at[:, pl.ds(col, width)], sem)
    copy.start()
    return copy


def column_kernel(bits, pieces, todo, fresh, *refs):
    own, others = todo
    me, grp = lax.axis_index("seq"), lax.axis_index("grp")
    if own:
        mine, *refs = refs
    if others:
        other, *refs = refs
    shard_refs = []
    for spots, _ in pieces:
        shard_refs.append([ref if at is None else ref.at[at] for at, ref in zip(spots, refs)])
        refs = refs[len(spots) :]
    if own:
        out, *refs = refs[0 if fresh else 1 :]
    if others:
        away, *refs = refs
    weight, *refs = refs
    if own:
        tile, sems = refs
    copies = []
    for k, (bit, parts) in enumerate(zip(bits, shard_refs)):
        if len(parts) == 1:
            (whole,) = parts
        else:
            whole = weight.at[k]
            rows = parts[0].shape[0]
            for part, half in zip(parts, (grp, 1 - grp) if pieces[k][1] else (0, 1)):
                whole[pl.ds(pl.multiple_of(half * rows, rows), rows), :] = part[...]
        if own:
            made = lax.dot_general(mine[...], whole[...], LAST, preferred_element_type=F32)
            tile[k] = made.astype(BF16)
            copies.append(put(tile.at[k], out, me ^ bit, sems.at[k]))
        if others:
            made = lax.dot_general(other[...], whole[...], LAST, preferred_element_type=F32)
            away[k] = made.astype(BF16)
    for copy in copies:
        copy.wait()


def columns(name, bits, mine, other, shards, out, out_shape):
    own, others = mine is not None, other is not None
    vmem, hbm = pl.BlockSpec(memory_space=VMEM), pl.BlockSpec(memory_space=pltpu.HBM)
    split_parts = [[p if isinstance(p, tuple) else (p, None) for p in shard[0]] for shard in shards]
    pieces = [([at for _, at in parts], shard[1]) for parts, shard in zip(split_parts, shards)]
    tokens = [t for t in (mine, other) if t is not None]
    operands = [*tokens, *(array for parts in split_parts for array, _ in parts)]
    in_specs = [vmem] * len(operands)
    count, height = len(shards), out_shape[0]
    rows, depth = sum(array.shape[-2] for array, _ in split_parts[0]), tokens[0].shape[1]
    tall = (count, height, rows)
    out_specs, shapes, scratch, aliases = [], [], [VMEM((count, rows, depth), BF16)], {}
    if own:
        out_specs.append(hbm)
        shapes.append(jax.ShapeDtypeStruct(out_shape, BF16))
        scratch += [VMEM(tall, BF16), pltpu.SemaphoreType.DMA((count,))]
        if out is not None:
            aliases = {len(operands): 0}
            operands.append(out)
            in_specs.append(hbm)
    if others:
        out_specs.append(vmem)
        shapes.append(jax.ShapeDtypeStruct(tall, BF16))
    return pl.pallas_call(
        functools.partial(column_kernel, bits, pieces, (own, others), out is None),
        in_specs=in_specs,
        out_specs=out_specs,
        out_shape=shapes,
        scratch_shapes=scratch,
        input_output_aliases=aliases,
        compiler_params=params(),
        cost_estimate=SMALL,
        name=name,
    )(*operands)


def place_kernel(bits, ids, *refs):
    (*came, _, out, tiles, sems) = refs
    me = lax.axis_index("seq")
    live = jnp.sum((ids[...] != 0).astype(jnp.int32))
    row = lax.broadcasted_iota(jnp.int32, tiles.shape[1:], 0)
    copies = []
    given = [ref.at[k] for ref in came for k in range(ref.shape[0])]
    for n, (bit, ref) in enumerate(zip(bits, given)):
        tiles[n] = jnp.where(row < live, ref[...].astype(F32), 0.0).astype(BF16)
        copies.append(put(tiles.at[n], out, me ^ bit, sems.at[n]))
    for copy in copies:
        copy.wait()


def place_columns(bits, token_ids, came, out):
    vmem, hbm = pl.BlockSpec(memory_space=VMEM), pl.BlockSpec(memory_space=pltpu.HBM)
    return pl.pallas_call(
        functools.partial(place_kernel, bits),
        in_specs=[vmem] * (1 + len(came)) + [hbm],
        out_specs=hbm,
        out_shape=jax.ShapeDtypeStruct(out.shape, BF16),
        scratch_shapes=[
            VMEM((len(bits), *came[0].shape[1:]), BF16),
            pltpu.SemaphoreType.DMA((len(bits),)),
        ],
        input_output_aliases={1 + len(came): 0},
        compiler_params=params(),
        cost_estimate=SMALL,
        name="place_columns",
    )(token_ids, *came, out)


def swap(value, axis, size, bits):
    return lax.ppermute(value, axis, [(i, i ^ bits) for i in range(size)])


def by_exchange(
    size, hidden, token_ids, upstream, w_value, proj_in, proj_out, in_inverse, out_inverse, datastore
):
    ring = functools.partial(lambda bits, v: swap(v, "seq", size, bits))
    core, side = 1, 2
    far = [4 * k for k in range(1, size // 4)]
    cross = lambda v: swap(v, "grp", 2, 1)
    me, grp = lax.axis_index("seq"), lax.axis_index("grp")
    half = w_value.shape[0] // 2
    out_shape = (hidden.shape[0], w_value.shape[0] * size)
    own_half = lambda v: lax.dynamic_slice_in_dim(v, grp * half, half, 0)
    after = lambda v, *first: lax.optimization_barrier((v, *first))[0]

    with jax.named_scope("weight_first"):
        upstream_other = ring(core, upstream)
        near = own_half(w_value)
        beside, h4, h8 = ring(side, w_value), ring(4, near), ring(8, near)
    masked, grad = query_gradient(
        token_ids, upstream, hidden, proj_in, proj_out, in_inverse, out_inverse
    )
    stages = [[0, side], [4, 8], [12, 4 ^ side, 8 ^ side], [12 ^ side]]
    shards = {0: ((w_value,), False)}

    def stage_columns(n, out, mine=True, other=True):
        with jax.named_scope("input_grad"):
            made = columns(
                f"columns_{n}",
                stages[n],
                masked if mine else None,
                upstream_other if other else None,
                [shards[b] for b in stages[n]],
                out,
                out_shape,
            )
            return [*made[:-1], ring(core, made[-1])] if other else made

    with jax.named_scope("weight_second"):
        h4, h8, beside = after((h4, h8, beside), grad)
        both = pair_up(h4, h8)
        x48, y48, h12 = cross(both), ring(side, both), ring(4, h8)

    shards[side] = (beside,), False
    out, back = stage_columns(0, None)
    came_back = [back]

    with jax.named_scope("query_exchange"):
        held, order = after(grad, upstream_other), [0]
        for bit in (8, side):
            came = ring(bit, held)
            if bit == side:
                held, came, x48, y48, h12, out = lax.optimization_barrier(
                    (held, came, x48, y48, h12, out)
                )
            held, order = join(held, came), order + [b ^ bit for b in order]
        shards.update({4: ((h4, (x48, 0)), True), 8: ((h8, (x48, 1)), True)})
        came = ring(4, held)
        cut = came.shape[0] // 2
        groups = [held, came, ring(core, held), ring(core, came[:cut]), ring(core, came[cut:])]
        order = [b ^ s for s in (0, 4, core, 4 ^ core) for b in order]
    raw, power = raw_score_call(order, groups, datastore)

    with jax.named_scope("weight_third"):
        x12, y12 = cross(pair_up(h12, (y48, 0))), ring(side, pair_up(h12, (x48, 1)))

    out, back = stage_columns(1, after(out, power))
    came_back.append(back)
    with jax.named_scope("power"):
        for bit in (core, side, 4, 8):
            part = ring(bit, power)
            if bit == side:
                part, out, x12, y12 = lax.optimization_barrier((part, out, x12, y12))
                shards[12] = (h12, (x12, 0)), True
                shards[4 ^ side] = ((y48, 0), (x12, 1)), True
                shards[8 ^ side] = ((y48, 1), (y12, 1)), True
                d12 = cross(y12[0])
                came_back += stage_columns(2, out, mine=False)
                (out,) = stage_columns(2, out, other=False)
            if bit == 8:
                part, out, d12 = lax.optimization_barrier((part, out, d12))
            power = power + part
        spread = jnp.sqrt(power[:, :1] / (datastore.shape[0] * size) + 1e-06)

    shards[12 ^ side] = ((y12, 0), d12), True
    came_back += stage_columns(3, out, mine=False)
    (out,) = stage_columns(3, out, other=False)
    out = place_columns([core ^ b for stage in stages for b in stage], token_ids, came_back, out)
    return out, raw / spread


def by_gather(
    size, hidden, token_ids, upstream, w_value, proj_in, proj_out, in_inverse, out_inverse, datastore
):
    queries, seq_tokens = token_ids.shape
    heads, head_dim, rank = proj_out.shape
    live_mask = (token_ids != 0).reshape(-1, 1).astype(BF16)
    masked = upstream * live_mask
    full_weight = lax.all_gather(w_value, "seq", axis=0, tiled=True)
    input_grad = lax.dot_general(masked, full_weight, LAST, preferred_element_type=F32).astype(BF16)
    left = jnp.dot(hidden, proj_in, preferred_element_type=F32).astype(BF16)
    right = jnp.einsum(
        "thd,hdr->thr", masked.reshape(-1, heads, head_dim), proj_out, preferred_element_type=F32
    ).astype(BF16)
    raw_grads = jnp.einsum(
        "qti,qthj->qhij",
        left.reshape(queries, seq_tokens, rank),
        right.reshape(queries, seq_tokens, heads, rank),
        preferred_element_type=F32,
    )
    half_way = jnp.einsum("hai,qhij->qhaj", in_inverse, raw_grads, precision=HIGHEST)
    pre = jnp.einsum("qhaj,hjb->qhab", half_way, out_inverse, precision=HIGHEST)
    grads = pre.astype(BF16).reshape(queries, -1)
    raw = lax.dot_general(
        lax.all_gather(grads, "seq", axis=0, tiled=True),
        datastore,
        LAST,
        preferred_element_type=F32,
    )
    power = lax.psum(jnp.sum(raw * raw, axis=1), "seq")
    spread = jnp.sqrt(power / (datastore.shape[0] * size) + 1e-06)
    return input_grad, raw / spread[:, None]


def solution(mesh):
    size, groups = mesh.shape["seq"], mesh.shape["grp"]

    def on_device(*args):
        hidden, token_ids, upstream, w_value = args[:4]
        fits = (
            groups == 2
            and size == 16
            and token_ids.shape[0] == 1
            and w_value.shape[0] % 256 == 0
        )
        return (by_exchange if fits else by_gather)(size, *args)

    rows = P(("grp", "seq"), None)
    return jax.shard_map(
        on_device,
        mesh=mesh,
        in_specs=(rows, rows, rows, P("seq", None), P(), P(), P(), P(), rows),
        out_specs=(rows, P("grp", "seq")),
        check_vma=False,
    )
```

```python
import functools

import jax
import jax.numpy as jnp
from jax import lax
from jax.experimental import pallas as pl
from jax.experimental.pallas import tpu as pltpu
from jax.sharding import PartitionSpec as P

BF16 = jnp.bfloat16
F32 = jnp.float32
HIGHEST = lax.Precision.HIGHEST
LAST = (((1,), (1,)), ((), ()))
FIRST = (((0,), (0,)), ((), ()))
VMEM = pltpu.VMEM
MIB = 1024 * 1024


SMALL = pl.CostEstimate(flops=1, bytes_accessed=1, transcendentals=0)


def params(mib=24):
    return pltpu.CompilerParams(vmem_limit_bytes=mib * MIB)


def split(x):
    high = x.astype(BF16)
    return high, (x - high.astype(F32)).astype(BF16)


def mask_kernel(ids, up, masked):
    live = jnp.sum((ids[...] != 0).astype(jnp.int32))
    row = lax.broadcasted_iota(jnp.int32, up.shape, 0)
    masked[...] = jnp.where(row < live, up[...].astype(F32), 0.0).astype(BF16)


def grad_kernel(ids, pout, a_inv, b_inv, up_hbm, hid_hbm, pin_hbm, masked, grad, up, hid, pin, sems):
    steps, _, chunk = hid.shape
    copies = [pltpu.make_async_copy(pin_hbm, pin, sems.at[0])]
    for k in range(steps):
        copies.append(
            pltpu.make_async_copy(hid_hbm.at[:, pl.ds(k * chunk, chunk)], hid.at[k], sems.at[1 + k])
        )
    copies.append(pltpu.make_async_copy(up_hbm, up, sems.at[1 + steps]))
    for copy in copies:
        copy.start()
    heads, rank, head_dim = pout.shape
    half = rank // 2
    out_sides, in_sides = [], []
    for h in range(heads):
        high, low = split(b_inv[h])
        side = lax.dot_general(pout[h], high, FIRST, preferred_element_type=F32)
        side += lax.dot_general(pout[h], low, FIRST, preferred_element_type=F32)
        high, low = split(side)
        out_sides.append(jnp.concatenate([high, low, high], axis=0))
        rows = [a_inv[h, pl.ds(odd, half, stride=2), :] for odd in range(2)]
        high, low = split(jnp.concatenate(rows, axis=0))
        in_sides.append(jnp.concatenate([high, high, low], axis=1))
    copies[0].wait()
    left = None
    for k in range(steps):
        copies[1 + k].wait()
        part = lax.dot_general(
            hid[k], pin[:, k * chunk : (k + 1) * chunk], LAST, preferred_element_type=F32
        )
        left = part if left is None else left + part
    copies[-1].wait()
    mask_kernel(ids, up, masked)
    both = jnp.dot(left.T.astype(BF16), masked[...], preferred_element_type=F32)
    high, low = split(both)
    for h in range(heads):
        lanes = slice(h * head_dim, (h + 1) * head_dim)
        terms = jnp.concatenate([high[:, lanes], high[:, lanes], low[:, lanes]], axis=1)
        mid = jnp.dot(terms, out_sides[h], preferred_element_type=F32)
        mid_high, mid_low = split(mid)
        terms = jnp.concatenate([mid_high, mid_low, mid_high], axis=0)
        pre = jnp.dot(in_sides[h], terms, preferred_element_type=F32)
        grad[0, h * half : (h + 1) * half, :] = jnp.concatenate(
            [pre[:half], pre[half:]], axis=1
        ).astype(BF16)


def query_gradient(token_ids, upstream, hidden, proj_in, proj_out, in_inverse, out_inverse):
    tokens, width = hidden.shape
    heads, head_dim, rank = proj_out.shape
    steps = 4 if width % 512 == 0 else 1
    vmem, hbm = pl.BlockSpec(memory_space=VMEM), pl.BlockSpec(memory_space=pltpu.HBM)
    whole = pl.BlockSpec()
    return pl.pallas_call(
        grad_kernel,
        in_specs=[whole] * 4 + [hbm] * 3,
        out_specs=[vmem, vmem],
        out_shape=[
            jax.ShapeDtypeStruct(upstream.shape, BF16),
            jax.ShapeDtypeStruct((1, heads * rank // 2, 2 * rank), BF16),
        ],
        scratch_shapes=[
            VMEM(upstream.shape, BF16),
            VMEM((steps, tokens, width // steps), BF16),
            VMEM((rank, width), BF16),
            pltpu.SemaphoreType.DMA((steps + 2,)),
        ],
        compiler_params=params(57),
        cost_estimate=SMALL,
        name="query_gradient",
    )(token_ids, proj_out.swapaxes(1, 2), in_inverse, out_inverse, upstream, hidden, proj_in.T)


def join_kernel(first, second, both):
    count = first.shape[0]
    both[:count] = first[...]
    both[count:] = second[...]


def join(first, second):
    vmem = pl.BlockSpec(memory_space=VMEM)
    shape = (first.shape[0] + second.shape[0], *first.shape[1:])
    return pl.pallas_call(
        join_kernel,
        in_specs=[vmem, vmem],
        out_specs=vmem,
        out_shape=jax.ShapeDtypeStruct(shape, first.dtype),
        compiler_params=params(),
        cost_estimate=SMALL,
        name="join",
    )(first, second)


def pair_kernel(spots, first, second, both):
    for n, (at, ref) in enumerate(zip(spots, (first, second))):
        both[n] = ref[...] if at is None else ref[at]


def pair_up(first, second):
    given = [p if isinstance(p, tuple) else (p, None) for p in (first, second)]
    vmem = pl.BlockSpec(memory_space=VMEM)
    shape = (2, *given[0][0].shape[-2:])
    return pl.pallas_call(
        functools.partial(pair_kernel, [at for _, at in given]),
        in_specs=[vmem, vmem],
        out_specs=vmem,
        out_shape=jax.ShapeDtypeStruct(shape, given[0][0].dtype),
        compiler_params=params(),
        cost_estimate=SMALL,
        name="pair_up",
    )(*(array for array, _ in given))


def score_kernel(bits, *refs):
    *held, store_hbm, scores, power, wide, store, sems = refs
    steps, _, chunk = store.shape
    copies = []
    for k in range(steps):
        copies.append(
            pltpu.make_async_copy(store_hbm.at[:, pl.ds(k * chunk, chunk)], store.at[k], sems.at[k])
        )
        copies[-1].start()
    me = lax.axis_index("seq")
    queries = len(bits)
    groups, lanes = held[0].shape[1:]
    rows = [ref.at[k] for ref in held for k in range(ref.shape[0])]
    for bit, row in zip(bits, rows):
        wide[pl.ds(me ^ bit, groups, stride=queries), :] = row[...].astype(F32)
    total = jnp.zeros(scores.shape, F32)
    each = chunk // lanes
    for k in range(steps):
        lhs = jnp.concatenate(
            [
                wide[g * queries : (g + 1) * queries, :].astype(BF16)
                for g in range(k * each, (k + 1) * each)
            ],
            axis=1,
        )
        copies[k].wait()
        total += lax.dot_general(lhs, store[k], LAST, preferred_element_type=F32)
    scores[...] = total
    square = jnp.sum(total * total, axis=1, keepdims=True)
    power[...] = jnp.broadcast_to(square, power.shape)


def raw_score_call(bits, held, datastore):
    groups, lanes = held[0].shape[1:]
    queries, (rows, flat) = len(bits), datastore.shape
    steps = 4 if groups % 4 == 0 else 1
    vmem = pl.BlockSpec(memory_space=VMEM)
    return pl.pallas_call(
        functools.partial(score_kernel, bits),
        in_specs=[vmem] * len(held) + [pl.BlockSpec(memory_space=pltpu.HBM)],
        out_specs=[vmem, vmem],
        out_shape=[
            jax.ShapeDtypeStruct((queries, rows), F32),
            jax.ShapeDtypeStruct((queries, lanes), F32),
        ],
        scratch_shapes=[
            VMEM((groups * queries, lanes), F32),
            VMEM((steps, rows, flat // steps), BF16),
            pltpu.SemaphoreType.DMA((steps,)),
        ],
        compiler_params=params(48),
        cost_estimate=SMALL,
        name="raw_scores",
    )(*held, datastore)


def put(source, out, spot, sem):
    width = source.shape[1]
    col = pl.multiple_of(spot * width, width)
    copy = pltpu.make_async_copy(source, out.at[:, pl.ds(col, width)], sem)
    copy.start()
    return copy


def column_kernel(bits, pieces, todo, fresh, *refs):
    own, others = todo
    me, grp = lax.axis_index("seq"), lax.axis_index("grp")
    if own:
        mine, *refs = refs
    if others:
        other, *refs = refs
    shard_refs = []
    for spots, _ in pieces:
        shard_refs.append([ref if at is None else ref.at[at] for at, ref in zip(spots, refs)])
        refs = refs[len(spots) :]
    if own:
        out, *refs = refs[0 if fresh else 1 :]
    if others:
        away, *refs = refs
    weight, *refs = refs
    if own:
        tile, sems = refs
    copies = []
    for k, (bit, parts) in enumerate(zip(bits, shard_refs)):
        if len(parts) == 1:
            (whole,) = parts
        else:
            whole = weight.at[k]
            rows = parts[0].shape[0]
            for part, half in zip(parts, (grp, 1 - grp) if pieces[k][1] else (0, 1)):
                whole[pl.ds(pl.multiple_of(half * rows, rows), rows), :] = part[...]
        if own:
            made = lax.dot_general(mine[...], whole[...], LAST, preferred_element_type=F32)
            tile[k] = made.astype(BF16)
            copies.append(put(tile.at[k], out, me ^ bit, sems.at[k]))
        if others:
            made = lax.dot_general(other[...], whole[...], LAST, preferred_element_type=F32)
            away[k] = made.astype(BF16)
    for copy in copies:
        copy.wait()


def columns(name, bits, mine, other, shards, out, out_shape):
    own, others = mine is not None, other is not None
    vmem, hbm = pl.BlockSpec(memory_space=VMEM), pl.BlockSpec(memory_space=pltpu.HBM)
    split_parts = [[p if isinstance(p, tuple) else (p, None) for p in shard[0]] for shard in shards]
    pieces = [([at for _, at in parts], shard[1]) for parts, shard in zip(split_parts, shards)]
    tokens = [t for t in (mine, other) if t is not None]
    operands = [*tokens, *(array for parts in split_parts for array, _ in parts)]
    in_specs = [vmem] * len(operands)
    count, height = len(shards), out_shape[0]
    rows, depth = sum(array.shape[-2] for array, _ in split_parts[0]), tokens[0].shape[1]
    tall = (count, height, rows)
    out_specs, shapes, scratch, aliases = [], [], [VMEM((count, rows, depth), BF16)], {}
    if own:
        out_specs.append(hbm)
        shapes.append(jax.ShapeDtypeStruct(out_shape, BF16))
        scratch += [VMEM(tall, BF16), pltpu.SemaphoreType.DMA((count,))]
        if out is not None:
            aliases = {len(operands): 0}
            operands.append(out)
            in_specs.append(hbm)
    if others:
        out_specs.append(vmem)
        shapes.append(jax.ShapeDtypeStruct(tall, BF16))
    return pl.pallas_call(
        functools.partial(column_kernel, bits, pieces, (own, others), out is None),
        in_specs=in_specs,
        out_specs=out_specs,
        out_shape=shapes,
        scratch_shapes=scratch,
        input_output_aliases=aliases,
        compiler_params=params(),
        cost_estimate=SMALL,
        name=name,
    )(*operands)


def place_kernel(bits, rows_in_all, ids, *refs):
    if rows_in_all:
        raw, power, *refs = refs
        *refs, out, scores, tiles, sems = refs
    else:
        *refs, out, tiles, sems = refs
    came = refs[:-1]
    me = lax.axis_index("seq")
    live = jnp.sum((ids[...] != 0).astype(jnp.int32))
    row = lax.broadcasted_iota(jnp.int32, tiles.shape[1:], 0)
    copies = []
    given = [ref.at[k] for ref in came for k in range(ref.shape[0])]
    for n, (bit, ref) in enumerate(zip(bits, given)):
        tiles[n] = jnp.where(row < live, ref[...].astype(F32), 0.0).astype(BF16)
        copies.append(put(tiles.at[n], out, me ^ bit, sems.at[n]))
    if rows_in_all:
        scores[...] = raw[...] / jnp.sqrt(power[:, : raw.shape[1]] / rows_in_all + 1e-06)
    for copy in copies:
        copy.wait()


def place_columns(bits, token_ids, came, out, raw=None, power=None, rows_in_all=0):
    vmem, hbm = pl.BlockSpec(memory_space=VMEM), pl.BlockSpec(memory_space=pltpu.HBM)
    extra = [raw, power] if rows_in_all else []
    shapes = [jax.ShapeDtypeStruct(out.shape, BF16)]
    if rows_in_all:
        shapes.append(jax.ShapeDtypeStruct(raw.shape, F32))
    return pl.pallas_call(
        functools.partial(place_kernel, bits, rows_in_all),
        in_specs=[vmem] * (1 + len(extra) + len(came)) + [hbm],
        out_specs=[hbm] + [vmem] * (len(shapes) - 1),
        out_shape=shapes,
        scratch_shapes=[
            VMEM((len(bits), *came[0].shape[1:]), BF16),
            pltpu.SemaphoreType.DMA((len(bits),)),
        ],
        input_output_aliases={1 + len(extra) + len(came): 0},
        compiler_params=params(),
        cost_estimate=SMALL,
        name="place_columns",
    )(token_ids, *extra, *came, out)


def swap(value, axis, size, bits):
    return lax.ppermute(value, axis, [(i, i ^ bits) for i in range(size)])


def by_exchange(
    size, hidden, token_ids, upstream, w_value, proj_in, proj_out, in_inverse, out_inverse, datastore
):
    ring = functools.partial(lambda bits, v: swap(v, "seq", size, bits))
    core, side = 1, 2
    far = [4 * k for k in range(1, size // 4)]
    cross = lambda v: swap(v, "grp", 2, 1)
    me, grp = lax.axis_index("seq"), lax.axis_index("grp")
    half = w_value.shape[0] // 2
    out_shape = (hidden.shape[0], w_value.shape[0] * size)
    own_half = lambda v: lax.dynamic_slice_in_dim(v, grp * half, half, 0)
    after = lambda v, *first: lax.optimization_barrier((v, *first))[0]

    with jax.named_scope("weight_first"):
        upstream_other = ring(core, upstream)
        near = own_half(w_value)
        beside, h4, h8 = ring(side, w_value), ring(4, near), ring(8, near)
    masked, grad = query_gradient(
        token_ids, upstream, hidden, proj_in, proj_out, in_inverse, out_inverse
    )
    stages = [[0, side], [4, 8], [12, 4 ^ side, 8 ^ side], [12 ^ side]]
    shards = {0: ((w_value,), False)}

    def stage_columns(n, out, mine=True, other=True):
        with jax.named_scope("input_grad"):
            made = columns(
                f"columns_{n}",
                stages[n],
                masked if mine else None,
                upstream_other if other else None,
                [shards[b] for b in stages[n]],
                out,
                out_shape,
            )
            return [*made[:-1], ring(core, made[-1])] if other else made

    with jax.named_scope("weight_second"):
        h4, h8 = after((h4, h8), grad)
        both = pair_up(h4, h8)
        x48, y48, h12 = cross(both), ring(side, both), ring(4, h8)

    shards[side] = (beside,), False
    out, back = stage_columns(0, None)
    came_back = [back]

    with jax.named_scope("query_exchange"):
        held, order = after(grad, upstream_other), [0]
        for bit in (8, side):
            came = ring(bit, held)
            if bit == side:
                held, came, x48, y48, h12, out = lax.optimization_barrier(
                    (held, came, x48, y48, h12, out)
                )
            held, order = join(held, came), order + [b ^ bit for b in order]
        shards.update({4: ((h4, (x48, 0)), True), 8: ((h8, (x48, 1)), True)})
        came = ring(4, held)
        cut = came.shape[0] // 2
        groups = [held, came, ring(core, held), ring(core, came[:cut]), ring(core, came[cut:])]
        order = [b ^ s for s in (0, 4, core, 4 ^ core) for b in order]
    raw, power = raw_score_call(order, groups, datastore)

    with jax.named_scope("weight_third"):
        x12, y12 = cross(pair_up(h12, (y48, 0))), ring(side, pair_up(h12, (x48, 1)))

    out, back = stage_columns(1, after(out, power))
    came_back.append(back)
    with jax.named_scope("power"):
        for bit in (core, side, 4, 8):
            part = ring(bit, power)
            if bit == side:
                part, out, x12, y12 = lax.optimization_barrier((part, out, x12, y12))
                shards[12] = (h12, (x12, 0)), True
                shards[4 ^ side] = ((y48, 0), (x12, 1)), True
                shards[8 ^ side] = ((y48, 1), (y12, 1)), True
                d12 = cross(y12[0])
                came_back += stage_columns(2, out, mine=False)
                (out,) = stage_columns(2, out, other=False)
            if bit == 8:
                part, out, d12 = lax.optimization_barrier((part, out, d12))
            power = power + part

    shards[12 ^ side] = ((y12, 0), d12), True
    came_back += stage_columns(3, out, mine=False)
    (out,) = stage_columns(3, out, other=False)
    order = [core ^ b for stage in stages for b in stage]
    rows_in_all = datastore.shape[0] * size
    return place_columns(order, token_ids, came_back, out, raw, power, rows_in_all)


def by_gather(
    size, hidden, token_ids, upstream, w_value, proj_in, proj_out, in_inverse, out_inverse, datastore
):
    queries, seq_tokens = token_ids.shape
    heads, head_dim, rank = proj_out.shape
    live_mask = (token_ids != 0).reshape(-1, 1).astype(BF16)
    masked = upstream * live_mask
    full_weight = lax.all_gather(w_value, "seq", axis=0, tiled=True)
    input_grad = lax.dot_general(masked, full_weight, LAST, preferred_element_type=F32).astype(BF16)
    left = jnp.dot(hidden, proj_in, preferred_element_type=F32).astype(BF16)
    right = jnp.einsum(
        "thd,hdr->thr", masked.reshape(-1, heads, head_dim), proj_out, preferred_element_type=F32
    ).astype(BF16)
    raw_grads = jnp.einsum(
        "qti,qthj->qhij",
        left.reshape(queries, seq_tokens, rank),
        right.reshape(queries, seq_tokens, heads, rank),
        preferred_element_type=F32,
    )
    half_way = jnp.einsum("hai,qhij->qhaj", in_inverse, raw_grads, precision=HIGHEST)
    pre = jnp.einsum("qhaj,hjb->qhab", half_way, out_inverse, precision=HIGHEST)
    grads = pre.astype(BF16).reshape(queries, -1)
    raw = lax.dot_general(
        lax.all_gather(grads, "seq", axis=0, tiled=True),
        datastore,
        LAST,
        preferred_element_type=F32,
    )
    power = lax.psum(jnp.sum(raw * raw, axis=1), "seq")
    spread = jnp.sqrt(power / (datastore.shape[0] * size) + 1e-06)
    return input_grad, raw / spread[:, None]


def solution(mesh):
    size, groups = mesh.shape["seq"], mesh.shape["grp"]

    def on_device(*args):
        hidden, token_ids, upstream, w_value = args[:4]
        fits = (
            groups == 2
            and size == 16
            and token_ids.shape[0] == 1
            and w_value.shape[0] % 256 == 0
            and args[8].shape[0] <= 2 * args[4].shape[1]
        )
        return (by_exchange if fits else by_gather)(size, *args)

    rows = P(("grp", "seq"), None)
    return jax.shard_map(
        on_device,
        mesh=mesh,
        in_specs=(rows, rows, rows, P("seq", None), P(), P(), P(), P(), rows),
        out_specs=(rows, P("grp", "seq")),
        check_vma=False,
    )
```

```python
import functools

import jax
import jax.numpy as jnp
from jax import lax
from jax.experimental import pallas as pl
from jax.experimental.pallas import tpu as pltpu
from jax.sharding import PartitionSpec as P

BF16 = jnp.bfloat16
F32 = jnp.float32
HIGHEST = lax.Precision.HIGHEST
LAST = (((1,), (1,)), ((), ()))
FIRST = (((0,), (0,)), ((), ()))
VMEM = pltpu.VMEM
MIB = 1024 * 1024


SMALL = pl.CostEstimate(flops=1, bytes_accessed=1, transcendentals=0)


def params(mib=24):
    return pltpu.CompilerParams(vmem_limit_bytes=mib * MIB)


def split(x):
    high = x.astype(BF16)
    return high, (x - high.astype(F32)).astype(BF16)


def mask_kernel(ids, up, masked):
    live = jnp.sum((ids[...] != 0).astype(jnp.int32))
    row = lax.broadcasted_iota(jnp.int32, up.shape, 0)
    masked[...] = jnp.where(row < live, up[...].astype(F32), 0.0).astype(BF16)


def grad_kernel(ids, pout, a_inv, b_inv, up_hbm, hid_hbm, pin_hbm, masked, grad, up, hid, pin, sems):
    steps, _, chunk = hid.shape
    copies = [pltpu.make_async_copy(pin_hbm, pin, sems.at[0])]
    for k in range(steps):
        copies.append(
            pltpu.make_async_copy(hid_hbm.at[:, pl.ds(k * chunk, chunk)], hid.at[k], sems.at[1 + k])
        )
    copies.append(pltpu.make_async_copy(up_hbm, up, sems.at[1 + steps]))
    for copy in copies:
        copy.start()
    heads, rank, head_dim = pout.shape
    half = rank // 2
    out_sides, in_sides = [], []
    for h in range(heads):
        high, low = split(b_inv[h])
        side = lax.dot_general(pout[h], high, FIRST, preferred_element_type=F32)
        side += lax.dot_general(pout[h], low, FIRST, preferred_element_type=F32)
        high, low = split(side)
        out_sides.append(jnp.concatenate([high, low, high], axis=0))
        rows = [a_inv[h, pl.ds(odd, half, stride=2), :] for odd in range(2)]
        high, low = split(jnp.concatenate(rows, axis=0))
        in_sides.append(jnp.concatenate([high, high, low], axis=1))
    copies[0].wait()
    left = None
    for k in range(steps):
        copies[1 + k].wait()
        part = lax.dot_general(
            hid[k], pin[:, k * chunk : (k + 1) * chunk], LAST, preferred_element_type=F32
        )
        left = part if left is None else left + part
    copies[-1].wait()
    mask_kernel(ids, up, masked)
    both = jnp.dot(left.T.astype(BF16), masked[...], preferred_element_type=F32)
    high, low = split(both)
    for h in range(heads):
        lanes = slice(h * head_dim, (h + 1) * head_dim)
        terms = jnp.concatenate([high[:, lanes], high[:, lanes], low[:, lanes]], axis=1)
        mid = jnp.dot(terms, out_sides[h], preferred_element_type=F32)
        mid_high, mid_low = split(mid)
        terms = jnp.concatenate([mid_high, mid_low, mid_high], axis=0)
        pre = jnp.dot(in_sides[h], terms, preferred_element_type=F32)
        grad[0, h * half : (h + 1) * half, :] = jnp.concatenate(
            [pre[:half], pre[half:]], axis=1
        ).astype(BF16)


def query_gradient(token_ids, upstream, hidden, proj_in, proj_out, in_inverse, out_inverse):
    tokens, width = hidden.shape
    heads, head_dim, rank = proj_out.shape
    steps = 4 if width % 512 == 0 else 1
    vmem, hbm = pl.BlockSpec(memory_space=VMEM), pl.BlockSpec(memory_space=pltpu.HBM)
    whole = pl.BlockSpec()
    return pl.pallas_call(
        grad_kernel,
        in_specs=[whole] * 4 + [hbm] * 3,
        out_specs=[vmem, vmem],
        out_shape=[
            jax.ShapeDtypeStruct(upstream.shape, BF16),
            jax.ShapeDtypeStruct((1, heads * rank // 2, 2 * rank), BF16),
        ],
        scratch_shapes=[
            VMEM(upstream.shape, BF16),
            VMEM((steps, tokens, width // steps), BF16),
            VMEM((rank, width), BF16),
            pltpu.SemaphoreType.DMA((steps + 2,)),
        ],
        compiler_params=params(57),
        cost_estimate=SMALL,
        name="query_gradient",
    )(token_ids, proj_out.swapaxes(1, 2), in_inverse, out_inverse, upstream, hidden, proj_in.T)


def join_kernel(first, second, both):
    count = first.shape[0]
    both[:count] = first[...]
    both[count:] = second[...]


def near_copy_kernel(value, copied):
    copied[...] = value[...]


def near_copy(value):
    vmem = pl.BlockSpec(memory_space=VMEM)
    return pl.pallas_call(
        near_copy_kernel,
        in_specs=[vmem],
        out_specs=vmem,
        out_shape=jax.ShapeDtypeStruct(value.shape, value.dtype),
        compiler_params=params(),
        cost_estimate=SMALL,
        name="near_copy",
    )(value)


def join(first, second):
    vmem = pl.BlockSpec(memory_space=VMEM)
    shape = (first.shape[0] + second.shape[0], *first.shape[1:])
    return pl.pallas_call(
        join_kernel,
        in_specs=[vmem, vmem],
        out_specs=vmem,
        out_shape=jax.ShapeDtypeStruct(shape, first.dtype),
        compiler_params=params(),
        cost_estimate=SMALL,
        name="join",
    )(first, second)


def pair_kernel(spots, first, second, both):
    for n, (at, ref) in enumerate(zip(spots, (first, second))):
        both[n] = ref[...] if at is None else ref[at]


def pair_up(first, second):
    given = [p if isinstance(p, tuple) else (p, None) for p in (first, second)]
    vmem = pl.BlockSpec(memory_space=VMEM)
    shape = (2, *given[0][0].shape[-2:])
    return pl.pallas_call(
        functools.partial(pair_kernel, [at for _, at in given]),
        in_specs=[vmem, vmem],
        out_specs=vmem,
        out_shape=jax.ShapeDtypeStruct(shape, given[0][0].dtype),
        compiler_params=params(),
        cost_estimate=SMALL,
        name="pair_up",
    )(*(array for array, _ in given))


def score_kernel(bits, *refs):
    *held, store_hbm, scores, power, wide, store, sems = refs
    steps, _, chunk = store.shape
    copies = []
    for k in range(steps):
        copies.append(
            pltpu.make_async_copy(store_hbm.at[:, pl.ds(k * chunk, chunk)], store.at[k], sems.at[k])
        )
        copies[-1].start()
    me = lax.axis_index("seq")
    queries = len(bits)
    groups, lanes = held[0].shape[1:]
    rows = [ref.at[k] for ref in held for k in range(ref.shape[0])]
    for bit, row in zip(bits, rows):
        wide[pl.ds(me ^ bit, groups, stride=queries), :] = row[...].astype(F32)
    total = jnp.zeros(scores.shape, F32)
    each = chunk // lanes
    for k in range(steps):
        lhs = jnp.concatenate(
            [
                wide[g * queries : (g + 1) * queries, :].astype(BF16)
                for g in range(k * each, (k + 1) * each)
            ],
            axis=1,
        )
        copies[k].wait()
        total += lax.dot_general(lhs, store[k], LAST, preferred_element_type=F32)
    scores[...] = total
    square = jnp.sum(total * total, axis=1, keepdims=True)
    power[...] = jnp.broadcast_to(square, power.shape)


def raw_score_call(bits, held, datastore):
    groups, lanes = held[0].shape[1:]
    queries, (rows, flat) = len(bits), datastore.shape
    steps = 4 if groups % 4 == 0 else 1
    vmem = pl.BlockSpec(memory_space=VMEM)
    return pl.pallas_call(
        functools.partial(score_kernel, bits),
        in_specs=[vmem] * len(held) + [pl.BlockSpec(memory_space=pltpu.HBM)],
        out_specs=[vmem, vmem],
        out_shape=[
            jax.ShapeDtypeStruct((queries, rows), F32),
            jax.ShapeDtypeStruct((queries, lanes), F32),
        ],
        scratch_shapes=[
            VMEM((groups * queries, lanes), F32),
            VMEM((steps, rows, flat // steps), BF16),
            pltpu.SemaphoreType.DMA((steps,)),
        ],
        compiler_params=params(48),
        cost_estimate=SMALL,
        name="raw_scores",
    )(*held, datastore)


def put(source, out, spot, sem):
    width = source.shape[1]
    col = pl.multiple_of(spot * width, width)
    copy = pltpu.make_async_copy(source, out.at[:, pl.ds(col, width)], sem)
    copy.start()
    return copy


def column_kernel(bits, pieces, todo, fresh, *refs):
    own, others = todo
    me, grp = lax.axis_index("seq"), lax.axis_index("grp")
    if own:
        mine, *refs = refs
    if others:
        other, *refs = refs
    shard_refs = []
    for spots, _ in pieces:
        shard_refs.append([ref if at is None else ref.at[at] for at, ref in zip(spots, refs)])
        refs = refs[len(spots) :]
    if own:
        out, *refs = refs[0 if fresh else 1 :]
    if others:
        away, *refs = refs
    weight, *refs = refs
    if own:
        tile, sems = refs
    copies = []
    for k, (bit, parts) in enumerate(zip(bits, shard_refs)):
        if len(parts) == 1:
            (whole,) = parts
        else:
            whole = weight.at[k]
            rows = parts[0].shape[0]
            for part, half in zip(parts, (grp, 1 - grp) if pieces[k][1] else (0, 1)):
                whole[pl.ds(pl.multiple_of(half * rows, rows), rows), :] = part[...]
        if own:
            made = lax.dot_general(mine[...], whole[...], LAST, preferred_element_type=F32)
            tile[k] = made.astype(BF16)
            copies.append(put(tile.at[k], out, me ^ bit, sems.at[k]))
        if others:
            made = lax.dot_general(other[...], whole[...], LAST, preferred_element_type=F32)
            away[k] = made.astype(BF16)
    for copy in copies:
        copy.wait()


def columns(name, bits, mine, other, shards, out, out_shape):
    own, others = mine is not None, other is not None
    vmem, hbm = pl.BlockSpec(memory_space=VMEM), pl.BlockSpec(memory_space=pltpu.HBM)
    split_parts = [[p if isinstance(p, tuple) else (p, None) for p in shard[0]] for shard in shards]
    pieces = [([at for _, at in parts], shard[1]) for parts, shard in zip(split_parts, shards)]
    tokens = [t for t in (mine, other) if t is not None]
    operands = [*tokens, *(array for parts in split_parts for array, _ in parts)]
    in_specs = [vmem] * len(operands)
    count, height = len(shards), out_shape[0]
    rows, depth = sum(array.shape[-2] for array, _ in split_parts[0]), tokens[0].shape[1]
    tall = (count, height, rows)
    out_specs, shapes, scratch, aliases = [], [], [VMEM((count, rows, depth), BF16)], {}
    if own:
        out_specs.append(hbm)
        shapes.append(jax.ShapeDtypeStruct(out_shape, BF16))
        scratch += [VMEM(tall, BF16), pltpu.SemaphoreType.DMA((count,))]
        if out is not None:
            aliases = {len(operands): 0}
            operands.append(out)
            in_specs.append(hbm)
    if others:
        out_specs.append(vmem)
        shapes.append(jax.ShapeDtypeStruct(tall, BF16))
    return pl.pallas_call(
        functools.partial(column_kernel, bits, pieces, (own, others), out is None),
        in_specs=in_specs,
        out_specs=out_specs,
        out_shape=shapes,
        scratch_shapes=scratch,
        input_output_aliases=aliases,
        compiler_params=params(),
        cost_estimate=SMALL,
        name=name,
    )(*operands)


def place_kernel(bits, rows_in_all, ids, *refs):
    if rows_in_all:
        raw, power, *refs = refs
        *refs, out, scores, tiles, sems = refs
    else:
        *refs, out, tiles, sems = refs
    came = refs[:-1]
    me = lax.axis_index("seq")
    live = jnp.sum((ids[...] != 0).astype(jnp.int32))
    row = lax.broadcasted_iota(jnp.int32, tiles.shape[1:], 0)
    copies = []
    given = [ref.at[k] for ref in came for k in range(ref.shape[0])]
    for n, (bit, ref) in enumerate(zip(bits, given)):
        tiles[n] = jnp.where(row < live, ref[...].astype(F32), 0.0).astype(BF16)
        copies.append(put(tiles.at[n], out, me ^ bit, sems.at[n]))
    if rows_in_all:
        scores[...] = raw[...] / jnp.sqrt(power[:, : raw.shape[1]] / rows_in_all + 1e-06)
    for copy in copies:
        copy.wait()


def place_columns(bits, token_ids, came, out, raw=None, power=None, rows_in_all=0):
    vmem, hbm = pl.BlockSpec(memory_space=VMEM), pl.BlockSpec(memory_space=pltpu.HBM)
    extra = [raw, power] if rows_in_all else []
    shapes = [jax.ShapeDtypeStruct(out.shape, BF16)]
    if rows_in_all:
        shapes.append(jax.ShapeDtypeStruct(raw.shape, F32))
    return pl.pallas_call(
        functools.partial(place_kernel, bits, rows_in_all),
        in_specs=[vmem] * (1 + len(extra) + len(came)) + [hbm],
        out_specs=[hbm] + [vmem] * (len(shapes) - 1),
        out_shape=shapes,
        scratch_shapes=[
            VMEM((len(bits), *came[0].shape[1:]), BF16),
            pltpu.SemaphoreType.DMA((len(bits),)),
        ],
        input_output_aliases={1 + len(extra) + len(came): 0},
        compiler_params=params(),
        cost_estimate=SMALL,
        name="place_columns",
    )(token_ids, *extra, *came, out)


def swap(value, axis, size, bits):
    return lax.ppermute(value, axis, [(i, i ^ bits) for i in range(size)])


def by_exchange(
    size, hidden, token_ids, upstream, w_value, proj_in, proj_out, in_inverse, out_inverse, datastore
):
    ring = functools.partial(lambda bits, v: swap(v, "seq", size, bits))
    core, side = 1, 2
    far = [4 * k for k in range(1, size // 4)]
    cross = lambda v: swap(v, "grp", 2, 1)
    me, grp = lax.axis_index("seq"), lax.axis_index("grp")
    half = w_value.shape[0] // 2
    out_shape = (hidden.shape[0], w_value.shape[0] * size)
    own_half = lambda v: lax.dynamic_slice_in_dim(v, grp * half, half, 0)
    after = lambda v, *first: lax.optimization_barrier((v, *first))[0]

    with jax.named_scope("weight_first"):
        upstream_other = ring(core, upstream)
        near = own_half(w_value)
        h8, h4, beside = ring(8, near), ring(4, near), ring(side, w_value)
    masked, grad = query_gradient(
        token_ids, upstream, hidden, proj_in, proj_out, in_inverse, out_inverse
    )
    stages = [[0, side], [4, 8], [12, 4 ^ side, 8 ^ side], [12 ^ side]]
    shards = {0: ((w_value,), False)}

    def stage_columns(n, out, mine=True, other=True):
        with jax.named_scope("input_grad"):
            made = columns(
                f"columns_{n}",
                stages[n],
                masked if mine else None,
                upstream_other if other else None,
                [shards[b] for b in stages[n]],
                out,
                out_shape,
            )
            return [*made[:-1], ring(core, made[-1])] if other else made

    with jax.named_scope("weight_second"):
        h8, h4 = after((h8, h4), grad)
        both = pair_up(h8, h4)
        x84, y84, h12 = cross(both), ring(side, both), ring(4, h8)

    shards[side] = (beside,), False
    out, back = stage_columns(0, None)
    came_back = [back]

    with jax.named_scope("query_exchange"):
        held, order = after(grad, upstream_other), [0]
        for bit in (8, side):
            came = ring(bit, held)
            if bit == 8:
                held = near_copy(held)
            if bit == side:
                held, came, x84, y84, h12, out = lax.optimization_barrier(
                    (held, came, x84, y84, h12, out)
                )
            held, order = join(held, came), order + [b ^ bit for b in order]
        shards.update({4: ((h4, (x84, 1)), True), 8: ((h8, (x84, 0)), True)})
        came = ring(4, held)
        cut = came.shape[0] // 2
        groups = [held, came, ring(core, held), ring(core, came[:cut]), ring(core, came[cut:])]
        order = [b ^ s for s in (0, 4, core, 4 ^ core) for b in order]
    raw, power = raw_score_call(order, groups, datastore)

    with jax.named_scope("weight_third"):
        x12, y12 = cross(pair_up(h12, (y84, 1))), ring(side, pair_up(h12, (x84, 0)))

    out, back = stage_columns(1, after(out, power))
    came_back.append(back)
    with jax.named_scope("power"):
        for bit in (core, side, 4, 8):
            part = ring(bit, power)
            if bit == side:
                part, out, x12, y12 = lax.optimization_barrier((part, out, x12, y12))
                shards[12] = (h12, (x12, 0)), True
                shards[4 ^ side] = ((y84, 1), (x12, 1)), True
                shards[8 ^ side] = ((y84, 0), (y12, 1)), True
                d12 = cross(y12[0])
                came_back += stage_columns(2, out, mine=False)
                (out,) = stage_columns(2, out, other=False)
            if bit == 8:
                part, out, d12 = lax.optimization_barrier((part, out, d12))
            power = power + part

    shards[12 ^ side] = ((y12, 0), d12), True
    came_back += stage_columns(3, out, mine=False)
    (out,) = stage_columns(3, out, other=False)
    order = [core ^ b for stage in stages for b in stage]
    rows_in_all = datastore.shape[0] * size
    return place_columns(order, token_ids, came_back, out, raw, power, rows_in_all)


def by_gather(
    size, hidden, token_ids, upstream, w_value, proj_in, proj_out, in_inverse, out_inverse, datastore
):
    queries, seq_tokens = token_ids.shape
    heads, head_dim, rank = proj_out.shape
    live_mask = (token_ids != 0).reshape(-1, 1).astype(BF16)
    masked = upstream * live_mask
    full_weight = lax.all_gather(w_value, "seq", axis=0, tiled=True)
    input_grad = lax.dot_general(masked, full_weight, LAST, preferred_element_type=F32).astype(BF16)
    left = jnp.dot(hidden, proj_in, preferred_element_type=F32).astype(BF16)
    right = jnp.einsum(
        "thd,hdr->thr", masked.reshape(-1, heads, head_dim), proj_out, preferred_element_type=F32
    ).astype(BF16)
    raw_grads = jnp.einsum(
        "qti,qthj->qhij",
        left.reshape(queries, seq_tokens, rank),
        right.reshape(queries, seq_tokens, heads, rank),
        preferred_element_type=F32,
    )
    half_way = jnp.einsum("hai,qhij->qhaj", in_inverse, raw_grads, precision=HIGHEST)
    pre = jnp.einsum("qhaj,hjb->qhab", half_way, out_inverse, precision=HIGHEST)
    grads = pre.astype(BF16).reshape(queries, -1)
    raw = lax.dot_general(
        lax.all_gather(grads, "seq", axis=0, tiled=True),
        datastore,
        LAST,
        preferred_element_type=F32,
    )
    power = lax.psum(jnp.sum(raw * raw, axis=1), "seq")
    spread = jnp.sqrt(power / (datastore.shape[0] * size) + 1e-06)
    return input_grad, raw / spread[:, None]


def solution(mesh):
    size, groups = mesh.shape["seq"], mesh.shape["grp"]

    def on_device(*args):
        hidden, token_ids, upstream, w_value = args[:4]
        fits = (
            groups == 2
            and size == 16
            and token_ids.shape[0] == 1
            and w_value.shape[0] % 256 == 0
            and args[8].shape[0] <= 2 * args[4].shape[1]
        )
        return (by_exchange if fits else by_gather)(size, *args)

    rows = P(("grp", "seq"), None)
    return jax.shard_map(
        on_device,
        mesh=mesh,
        in_specs=(rows, rows, rows, P("seq", None), P(), P(), P(), P(), rows),
        out_specs=(rows, P("grp", "seq")),
        check_vma=False,
    )
```
